128 devices in a mesh: space: 16 (over x, z), chan: 8 (over y, core).
Axes of the slice: x: 4, y: 4, z: 4, core: 2. Of those that a mesh axis runs over, the one named last changes fastest.
Arguments:
- volume: bfloat16 [64, 16, 16, 512], P('space', 'chan'), may hold values from -6 to 6
- w_first: bfloat16 [27, 512, 1024], P(None, 'space', 'chan'), may hold values from -0.0546875 to 0.0546875
- b_first: float32 [1024], P('chan'), may hold values from -3 to 3
- w_second: bfloat16 [27, 1024, 1024], P(None, 'space', 'chan'), may hold values from -0.0390625 to 0.0390625
- b_second: float32 [1024], P('chan'), may hold values from -3 to 3
- cotangent: bfloat16 [64, 16, 16, 1024], P('space', None, None, 'chan'), may hold values from -6 to 6
Outputs:
- features: bfloat16 [64, 16, 16, 1024], P('space', None, None, 'chan')
- grad_input: float32 [64, 16, 16, 512], P('space', 'chan')
- grad_first: float32 [27, 512, 1024], P(None, 'space', 'chan')
- grad_second: float32 [27, 1024, 1024], P(None, 'space', 'chan')
The draws below stay inside these ranges and needn't reach their ends.
All inputs are finite; a program needn't handle non-finite values.
Results may differ from the reference program's by a relative error of at most 0.0054.
Values may be sent and summed in bfloat16 or wider, within the bound.
A program may use at most 512 MiB of HBM per device.

```python
import jax
import jax.numpy as jnp

CIN = 512
C1 = 1024
GY = 16
GZ = 16
NX = 64


def steps_of(stream_key, shape, shards, smallest, top_value):
    def one(position, blocks):
        heights = jax.random.uniform(jax.random.fold_in(jax.random.fold_in(stream_key, 6), position), (blocks,), jnp.float32, smallest / len(shards), top_value / len(shards))
        return jnp.repeat(jnp.exp(heights), shape[position] // blocks).reshape((-1,) + (1,) * (len(shape) - position - 1))

    factor_of = one(*shards[0])
    for cut in shards[1:]:
        factor_of = factor_of * one(*cut)
    return factor_of


def scatter_about(stream_key, dims, scale, most, split=(), dtype=jnp.bfloat16):
    drawn = jax.random.normal(stream_key, dims, jnp.float32) * scale
    if len(split) > 0:
        drawn = steps_of(stream_key, dims, split, -0.22, 0.18) * drawn
    return jnp.clip(drawn, min=-most, max=most).astype(dtype)


def setup_inputs(seed: int = 0) -> dict:
    key_of = jax.random.split(jax.random.key(seed), 7)
    return {
        "volume": scatter_about(key_of[0], (NX, GY, GZ, CIN), 1.0, 6.0, ((0, 16), (1, 8))),
        "w_first": scatter_about(key_of[1], (27, CIN, C1), (27 * CIN) ** -0.5, 0.0546875, ((1, 16), (2, 8))),
        "b_first": scatter_about(key_of[2], (C1,), 0.5, 3.0, ((0, 8),), jnp.float32),
        "w_second": scatter_about(key_of[3], (27, C1, C1), (27 * C1) ** -0.5, 0.0390625, ((1, 16), (2, 8))),
        "b_second": scatter_about(key_of[4], (C1,), 0.5, 3.0, ((0, 8),), jnp.float32),
        "cotangent": scatter_about(key_of[5], (NX, GY, GZ, C1), 1.0, 6.0, ((0, 16), (3, 8))),
    }


def pad_all(field):
    return jnp.pad(field, ((1, 1), (1, 1), (1, 1), (0, 0)))

def silu_slope(values):
    sigma = jax.nn.sigmoid(values)
    return sigma * (1.0 + values * (1.0 - sigma))

def convolve(padded, weights):
    span_x = padded.shape[0] - 2
    span_y = padded.shape[1] - 2
    span_z = padded.shape[2] - 2
    summed = jnp.zeros((span_x * span_y * span_z, weights.shape[2]), jnp.float32)
    for offset in range(27):
        a, b, c = (offset // 9, offset // 3 % 3, offset % 3)
        sliced = padded[a:a + span_x, b:b + span_y, c:c + span_z].reshape(-1, padded.shape[3])
        summed = summed + jnp.dot(sliced, weights[offset], preferred_element_type=jnp.float32)
    return summed.reshape(span_x, span_y, span_z, -1)

def convolve_back(padded, weights):
    span_x = padded.shape[0] - 2
    span_y = padded.shape[1] - 2
    span_z = padded.shape[2] - 2
    summed = jnp.zeros((span_x * span_y * span_z, weights.shape[1]), jnp.float32)
    for offset in range(27):
        a, b, c = (offset // 9, offset // 3 % 3, offset % 3)
        sliced = padded[2 - a:2 - a + span_x, 2 - b:2 - b + span_y, 2 - c:2 - c + span_z].reshape(-1, padded.shape[3])
        summed = summed + jnp.dot(sliced, weights[offset].T, preferred_element_type=jnp.float32)
    return summed.reshape(span_x, span_y, span_z, -1)

def weight_grad(padded, grads):
    span_x = grads.shape[1]
    span_y = grads.shape[2]
    span_z = grads.shape[3]
    flat_grads = grads.reshape(-1, grads.shape[4])
    results = []
    for offset in range(27):
        a, b, c = (offset // 9, offset // 3 % 3, offset % 3)
        sliced = padded[:, a:a + span_x, b:b + span_y, c:c + span_z].reshape(-1, padded.shape[4])
        results.append(jnp.dot(sliced.T, flat_grads, preferred_element_type=jnp.float32))
    return jnp.stack(results)

def reference(volume, w_first, b_first, w_second, b_second, cotangent):
    padded_in = pad_all(volume)
    pre_first = convolve(padded_in, w_first) + b_first
    hidden = jax.nn.silu(pre_first).astype(jnp.bfloat16)
    padded_hidden = pad_all(hidden)
    pre_second = convolve(padded_hidden, w_second) + b_second
    features = jax.nn.silu(pre_second).astype(jnp.bfloat16)
    adjoint_out = (cotangent.astype(jnp.float32) * silu_slope(pre_second)).astype(jnp.bfloat16)
    hidden_adjoint = convolve_back(pad_all(adjoint_out), w_second)
    adjoint_first = (hidden_adjoint * silu_slope(pre_first)).astype(jnp.bfloat16)
    grad_input = convolve_back(pad_all(adjoint_first), w_first)
    grad_first = weight_grad(padded_in[None], adjoint_first[None])
    grad_second = weight_grad(padded_hidden[None], adjoint_out[None])
    return (features, grad_input, grad_first, grad_second)
```

```python
import functools

import jax
import jax.numpy as jnp
from jax import lax
from jax.experimental import pallas as pl
from jax.experimental.pallas import tpu as pltpu
from jax.sharding import PartitionSpec as P

MESH = pl.DeviceIdType.MESH
BF = jnp.bfloat16
F32 = jnp.float32
VMEM_BYTES = 63 * 1024 * 1024
RING = (1, 3, 2)
HALVES = ((0, 14), (14, 13))


def place():
    s = lax.axis_index("space")
    c = lax.axis_index("chan")
    return s, c, lax.div(s, 4), lax.rem(s, 4), lax.div(c, 2), lax.rem(c, 2)


def send(src, dst, send_sem, recv_sem, target):
    return pltpu.make_async_remote_copy(
        src_ref=src,
        dst_ref=dst,
        send_sem=send_sem,
        recv_sem=recv_sem,
        device_id=target,
        device_id_type=MESH,
    )


def greet(s, c, x, z):
    barrier = pltpu.get_barrier_semaphore()

    def signal(space, chan):
        pl.semaphore_signal(barrier, inc=1, device_id=(space, chan), device_id_type=MESH)

    for d in (1, 2, 3):
        signal(lax.rem(x + d, 4) * 4 + z, c)
        signal(x * 4 + lax.rem(z + d, 4), c)
    for d in range(1, 8):
        signal(s, lax.rem(c + d, 8))

    @pl.when(s > 0)
    def _():
        signal(s - 1, c)

    @pl.when(s < 15)
    def _():
        signal(s + 1, c)

    inner = jnp.where(s > 0, 1, 0) + jnp.where(s < 15, 1, 0)
    pl.semaphore_wait(barrier, 13 + inner)


class Halo:
    def __init__(self, s, c, low_src, high_src, low_dst, high_dst, send_sem, recv_sem):
        self.s = s
        self.down = send(low_src, high_dst, send_sem.at[0], recv_sem.at[0], (jnp.maximum(s - 1, 0), c))
        self.up = send(high_src, low_dst, send_sem.at[1], recv_sem.at[1], (jnp.minimum(s + 1, 15), c))

    def start_down(self):
        pl.when(self.s > 0)(self.down.start)

    def start_up(self):
        pl.when(self.s < 15)(self.up.start)

    def start(self):
        self.start_down()
        self.start_up()

    def wait_recv(self):
        pl.when(self.s < 15)(self.down.wait_recv)
        pl.when(self.s > 0)(self.up.wait_recv)

    def wait_send(self):
        pl.when(self.s > 0)(self.down.wait_send)
        pl.when(self.s < 15)(self.up.wait_send)


class Gather:
    def __init__(self, own, full, x, z, c, send_sem, recv_sem):
        self.own, self.full, self.x, self.z, self.c = own, full, x, z, c
        self.send_sem, self.recv_sem = send_sem, recv_sem

    def copy(self, half, first, second, source_own, stage):
        k0, nk = HALVES[half]
        back1, back2 = (first, second)
        if stage == 1:
            o1, o2 = 0, 0
        else:
            o1, o2 = back1, 0
        if half == 0:
            ox, oz = lax.rem(self.x + 4 - o1, 4), self.z
            tx = lax.rem(self.x + back1, 4) if stage == 1 else self.x
            tz = self.z if stage == 1 else lax.rem(self.z + back2, 4)
        else:
            ox, oz = self.x, lax.rem(self.z + 4 - o1, 4)
            tz = lax.rem(self.z + back1, 4) if stage == 1 else self.z
            tx = self.x if stage == 1 else lax.rem(self.x + back2, 4)
        dst = self.full.at[pl.ds(k0, nk), ox, oz]
        src = self.own.at[pl.ds(k0, nk)] if source_own else dst
        index = first * 4 + second
        return send(
            src,
            dst,
            self.send_sem.at[half, index],
            self.recv_sem.at[half, index],
            (tx * 4 + tz, self.c),
        )

    def arrived(self, half, first, second):
        k0, nk = HALVES[half]
        if half == 0:
            ox, oz = lax.rem(self.x + 4 - first, 4), lax.rem(self.z + 4 - second, 4)
        else:
            oz, ox = lax.rem(self.z + 4 - first, 4), lax.rem(self.x + 4 - second, 4)
        region = self.full.at[pl.ds(k0, nk), ox, oz]
        index = first * 4 + second
        send(
            region,
            region,
            self.send_sem.at[half, index],
            self.recv_sem.at[half, index],
            (lax.rem(self.x + 1, 4) * 4 + self.z, self.c),
        ).wait_recv()

    def start_own(self):
        for d in RING:
            for half in (0, 1):
                self.copy(half, d, 0, True, 1).start()
        for d in RING:
            for half in (0, 1):
                self.copy(half, 0, d, True, 2).start()

    def forward(self, d):
        for half in (0, 1):
            self.arrived(half, d, 0)
            for e in RING:
                self.copy(half, d, e, False, 2).start()

    def wait_second(self):
        for d in range(4):
            for e in RING:
                for half in (0, 1):
                    self.arrived(half, d, e)

    def wait_send(self):
        for half in (0, 1):
            for d in RING:
                self.copy(half, d, 0, True, 1).wait_send()
            for d in range(4):
                for e in RING:
                    self.copy(half, d, e, d == 0, 2).wait_send()


class ChanGather:
    def __init__(self, region, s, y, core, y_send, y_recv, c_send, c_recv):
        self.region, self.s, self.y, self.core = region, s, y, core
        self.sems = (y_send, y_recv, c_send, c_recv)

    def to_y(self, d):
        block = self.region(self.y * 2 + self.core)
        y_send, y_recv, _, _ = self.sems
        return send(
            block, block, y_send.at[d], y_recv.at[d], (self.s, lax.rem(self.y + d, 4) * 2 + self.core)
        )

    def from_y(self, d):
        block = self.region(lax.rem(self.y + 4 - d, 4) * 2 + self.core)
        y_send, y_recv, _, _ = self.sems
        return send(
            block, block, y_send.at[d], y_recv.at[d], (self.s, lax.rem(self.y + d, 4) * 2 + self.core)
        )

    def sibling(self, d, other):
        core = (1 - self.core) if other else self.core
        block = self.region(lax.rem(self.y + 4 - d, 4) * 2 + core)
        _, _, c_send, c_recv = self.sems
        return send(block, block, c_send.at[d], c_recv.at[d], (self.s, self.y * 2 + 1 - self.core))

    def start_own(self):
        for d in RING:
            self.to_y(d).start()
        self.sibling(0, False).start()

    def forward(self):
        for d in RING:
            self.from_y(d).wait_recv()
            self.sibling(d, False).start()

    def finish(self):
        for d in range(4):
            self.sibling(d, True).wait_recv()

    def wait_send(self):
        for d in RING:
            self.to_y(d).wait_send()
        for d in range(4):
            self.sibling(d, False).wait_send()


def z_mask(last):
    row = lax.broadcasted_iota(jnp.int32, (256, 128), 0)
    return lax.rem(row, 16) != (15 if last else 0)


def behind(v):
    return jnp.where(z_mask(False), pltpu.roll(v, 1, 0), 0.0)


def ahead(v):
    return jnp.where(z_mask(True), pltpu.roll(v, 255, 0), 0.0)


def slope_of(v):
    sigma = jax.nn.sigmoid(v)
    return sigma * (1.0 + v * (1.0 - sigma))


def stack_shifts(v, xp, stacked, x0, y0, flipped):
    for k, shifted in enumerate((ahead(v), v, behind(v))):
        stacked[xp + x0, y0 : y0 + 16, :, k * 128 : (k + 1) * 128] = shifted.astype(BF).reshape(16, 16, 128)
        flipped[k * 128 : (k + 1) * 128, xp * 256 : (xp + 1) * 256] = shifted.T.astype(BF)


def dot(a, b):
    return jnp.dot(a, b, preferred_element_type=F32)


def convolve_pair(load, load_w, planes, acc):
    def step(j, _):
        a, b = lax.div(j, 3), lax.rem(j, 3)
        rows = jnp.concatenate([load(p + a, b) for p in planes], axis=0)
        filters = jnp.concatenate([load_w(3 * j + k) for k in range(3)], axis=1)
        acc[...] += dot(rows, filters)
        return 0

    acc[...] = jnp.zeros_like(acc)
    lax.fori_loop(0, 9, step, 0)


def plane_of(acc, index):
    rows = slice(index * 256, (index + 1) * 256)
    return behind(acc[rows, 0:128]) + acc[rows, 128:256] + ahead(acc[rows, 256:384])


def forward_kernel(
    vol, w1, b1, w2, b2, cot,
    feat, stacked, flipped, slope, u1_out, u2_out, w1_out, w2_out,
    u1, u2, f1, f2, acc,
    ag1_s, ag1_r, ag2_s, ag2_r, halo_s, halo_r, hh_s, hh_r, y_s, y_r, c_s, c_r, hy_s, hy_r, hc_s, hc_r, loc,
):
    s, c, x, z, y, core = place()
    u1[0] = jnp.zeros((18, 16, 512), BF)
    u1[5] = jnp.zeros((18, 16, 512), BF)
    for row in (0, 17):
        u1[1:5, row] = jnp.zeros((4, 16, 512), BF)

    def clear(b, _):
        u2[b, 0] = jnp.zeros((18, 16, 128), BF)
        u2[b, 5] = jnp.zeros((18, 16, 128), BF)
        for row in (0, 17):
            u2[b, 1:5, row] = jnp.zeros((4, 16, 128), BF)
        return 0

    lax.fori_loop(0, 8, clear, 0)
    rows_of = lambda cb: u1.at[:, pl.ds(1 + 2 * cb, 2)]
    locals_ = [
        pltpu.make_async_copy(vol, u1.at[1:5, pl.ds(1 + 2 * c, 2)], loc.at[0]),
        pltpu.make_async_copy(w1, f1.at[:, x, z], loc.at[1]),
        pltpu.make_async_copy(w2, f2.at[:, x, z], loc.at[2]),
    ]
    for copy in locals_:
        copy.start()
    greet(s, c, x, z)

    first = Gather(w1, f1, x, z, c, ag1_s, ag1_r)
    second = Gather(w2, f2, x, z, c, ag2_s, ag2_r)
    halo = Halo(
        s, c, vol.at[0], vol.at[3],
        u1.at[0, pl.ds(1 + 2 * c, 2)], u1.at[5, pl.ds(1 + 2 * c, 2)], halo_s, halo_r,
    )
    rows = ChanGather(rows_of, s, y, core, y_s, y_r, c_s, c_r)
    halo.start()
    first.start_own()
    locals_[0].wait()
    halo.wait_recv()
    rows.start_own()
    for d in RING:
        first.forward(d)
    second.start_own()
    rows.forward()
    rows.finish()
    locals_[1].wait()
    locals_[2].wait()
    first.wait_second()
    save_u1 = pltpu.make_async_copy(u1, u1_out, loc.at[3])
    save_w1 = pltpu.make_async_copy(f1, w1_out, loc.at[4])
    save_u1.start()
    save_w1.start()

    hidden_halo = Halo(
        s, c, u2.at[c, 1, 1:17], u2.at[c, 4, 1:17], u2.at[c, 0, 1:17], u2.at[c, 5, 1:17], hh_s, hh_r
    )
    for planes in ((0, 3), (1, 2)):
        convolve_pair(
            lambda p, b: u1[p, pl.ds(b, 16)].reshape(256, 512),
            lambda k: f1[k].reshape(512, 128),
            planes,
            acc,
        )
        for index, p in enumerate(planes):
            pre = plane_of(acc, index) + b1[...]
            slope[p] = slope_of(pre)
            u2[c, p + 1, 1:17] = (pre * jax.nn.sigmoid(pre)).astype(BF).reshape(16, 16, 128)
        if planes == (0, 3):
            hidden_halo.start()
    hidden_halo.wait_recv()
    channels = ChanGather(lambda cb: u2.at[cb, :, 1:17], s, y, core, hy_s, hy_r, hc_s, hc_r)
    channels.start_own()
    for d in RING:
        second.forward(d)
    channels.forward()
    channels.finish()
    second.wait_second()
    save_u2 = pltpu.make_async_copy(u2, u2_out, loc.at[5])
    save_w2 = pltpu.make_async_copy(f2, w2_out, loc.at[6])
    save_u2.start()
    save_w2.start()

    for planes in ((0, 3), (1, 2)):
        convolve_pair(
            lambda p, b: jnp.concatenate([u2[q, p, pl.ds(b, 16)].reshape(256, 128) for q in range(8)], axis=1),
            lambda k: f2[k].reshape(1024, 128),
            planes,
            acc,
        )
        for index, p in enumerate(planes):
            pre = plane_of(acc, index) + b2[...]
            feat[p] = (pre * jax.nn.sigmoid(pre)).astype(BF).reshape(16, 16, 128)
            adjoint = cot[p].reshape(256, 128).astype(F32) * slope_of(pre)
            stack_shifts(adjoint, p, stacked, 0, 0, flipped)
    halo.wait_send()
    hidden_halo.wait_send()
    rows.wait_send()
    channels.wait_send()
    first.wait_send()
    second.wait_send()
    for copy in (save_u1, save_w1, save_u2, save_w2):
        copy.wait()


class Scatter:
    def __init__(self, terms, got1, mid, got2, total, out, x, z, c, sems, flip):
        self.terms, self.got1, self.mid, self.got2 = terms, got1, mid, got2
        self.total, self.out = total, out
        self.x, self.z, self.c, self.flip = x, z, c, flip
        self.s1, self.r1, self.s2, self.r2 = sems

    def by_axis(self, j, act):
        x_first = lax.rem(j + self.flip, 2) == 0

        @pl.when(x_first)
        def _():
            act(True)

        @pl.when(jnp.logical_not(x_first))
        def _():
            act(False)

    def target(self, along_x, d):
        tx = lax.rem(self.x + d, 4) if along_x else self.x
        tz = self.z if along_x else lax.rem(self.z + d, 4)
        return tx, tz

    def stage1(self, j, d, x_first):
        tx, tz = self.target(x_first, d)
        src = self.terms.at[pl.ds(3 * j, 3), tx] if x_first else self.terms.at[pl.ds(3 * j, 3), :, tz]
        return send(
            src, self.got1.at[j, d - 1], self.s1.at[j, d - 1], self.r1.at[j, d - 1], (tx * 4 + tz, self.c)
        )

    def stage2(self, j, d, x_first):
        tx, tz = self.target(not x_first, d)
        src = self.mid.at[j, :, tz] if x_first else self.mid.at[j, :, tx]
        return send(
            src, self.got2.at[j, d - 1], self.s2.at[j, d - 1], self.r2.at[j, d - 1], (tx * 4 + tz, self.c)
        )

    def start1(self, j):
        def act(x_first):
            for d in RING:
                self.stage1(j, d, x_first).start()

        self.by_axis(j, act)

    def start2(self, j):
        def act(x_first):
            for d in RING:
                self.stage1(j, d, x_first).wait_recv()
            own = self.terms[pl.ds(3 * j, 3), self.x] if x_first else self.terms[pl.ds(3 * j, 3), :, self.z]
            value = own.astype(F32)
            for d in range(3):
                value = value + self.got1[j, d].astype(F32)
            self.total[...] = value
            self.mid[j] = value.astype(BF)
            self.out[pl.ds(3 * j, 3)] = self.total[:, self.z] if x_first else self.total[:, self.x]
            for d in RING:
                self.stage2(j, d, x_first).start()

        self.by_axis(j, act)

    def finish(self, j):
        def act(x_first):
            for d in RING:
                self.stage2(j, d, x_first).wait_recv()
            value = self.out[pl.ds(3 * j, 3)]
            for d in range(3):
                value = value + self.got2[j, d].astype(F32)
            self.out[pl.ds(3 * j, 3)] = value
            for d in RING:
                self.stage1(j, d, x_first).wait_send()
                self.stage2(j, d, x_first).wait_send()

        self.by_axis(j, act)


def every_chunk(act):
    def step(j, _):
        act(j)
        return 0

    lax.fori_loop(0, 9, step, 0)


def back_columns(stacked, load_w):
    total = None
    for a in range(3):
        rows = jnp.concatenate(
            [stacked[2 - a : 6 - a, 2 - b : 18 - b].reshape(1024, 384) for b in range(3)], axis=1
        )
        filters = jnp.concatenate([load_w(9 * a + k) for k in range(9)], axis=1)
        term = lax.dot_general(rows, filters, (((1,), (1,)), ((), ())), preferred_element_type=F32)
        total = term if total is None else total + term
    return total


def backward_kernel(
    stacked_in, flipped2, slope, u1_in, u2, w1_in, w2_in,
    grad_in, grad1, grad2,
    u1, f1, f2, adj2, adj1, flipped1,
    terms2, got2a, mid2, got2b, total2,
    terms1, got1a, mid1, got1b, total1,
    hid_own, hid_bf, hid_sib, hid_sum, hid_got,
    inp_own, inp_bf, inp_sib, inp_sum, inp_got,
    g2s1, g2r1, g2s2, g2r2, g1s1, g1r1, g1s2, g1r2,
    h2s, h2r, h1s, h1r, hss, hsr, hys, hyr, iss, isr, iys, iyr, loc,
):
    s, c, x, z, y, core = place()
    loads = [
        pltpu.make_async_copy(stacked_in, adj2.at[1:5, 1:17], loc.at[0]),
        pltpu.make_async_copy(w2_in, f2, loc.at[1]),
        pltpu.make_async_copy(u1_in, u1, loc.at[2]),
        pltpu.make_async_copy(w1_in, f1, loc.at[3]),
    ]
    for copy in loads:
        copy.start()
    for field in (adj2, adj1):
        for plane in (0, 5):
            field[plane] = jnp.zeros((18, 16, 384), BF)
        for row in (0, 17):
            field[1:5, row] = jnp.zeros((4, 16, 384), BF)
    greet(s, c, x, z)
    sibling = (s, y * 2 + 1 - core)

    halo2 = Halo(
        s, c, stacked_in.at[0], stacked_in.at[3], adj2.at[0, 1:17], adj2.at[5, 1:17], h2s, h2r
    )
    halo2.start()
    scatter2 = Scatter(
        terms2, got2a, mid2, got2b, total2, grad2, x, z, c, (g2s1, g2r1, g2s2, g2r2), 0
    )
    scatter1 = Scatter(
        terms1, got1a, mid1, got1b, total1, grad1, x, z, c, (g1s1, g1r1, g1s2, g1r2), 1
    )

    def second_chunk(j):
        a, b = lax.div(j, 3), lax.rem(j, 3)

        def block(n, _):
            fields = [u2[2 * n + q, pl.ds(a, 4), pl.ds(b, 16)].reshape(1024, 128) for q in range(2)]
            turned = dot(flipped2[...], jnp.concatenate(fields, axis=1)).T.astype(BF)
            for k in range(3):
                terms2[3 * j + k, n] = turned[:, k * 128 : (k + 1) * 128].reshape(4, 64, 128)
            return 0

        lax.fori_loop(0, 4, block, 0)
        scatter2.start1(j)

    every_chunk(second_chunk)
    for copy in loads:
        copy.wait()
    halo2.wait_recv()

    def hidden_to_sibling(n):
        return send(hid_bf.at[n, 1 - core], hid_sib.at[n], hss.at[n], hsr.at[n], sibling)

    def hidden_columns(n, _):
        value = back_columns(adj2, lambda k: f2[k, n].reshape(256, 128))
        low, high = value[:, :128], value[:, 128:]
        hid_bf[n, 0] = low.astype(BF)
        hid_bf[n, 1] = high.astype(BF)
        hid_own[n] = jnp.where(core == 0, low, high)
        hidden_to_sibling(n).start()
        return 0

    lax.fori_loop(0, 4, hidden_columns, 0)

    def hidden_to_y(d):
        n = lax.rem(y + d, 4)
        return send(hid_sum.at[n], hid_got.at[d - 1], hys.at[d - 1], hyr.at[d - 1], (s, n * 2 + core))

    for d in (1, 3, 2, 0):
        n = lax.rem(y + d, 4)
        hidden_to_sibling(n).wait_recv()
        pair = hid_own[n] + hid_sib[n].astype(F32)
        if d:
            hid_sum[n] = pair.astype(BF)
            hidden_to_y(d).start()
        else:
            hid_own[n] = pair
    for d in RING:
        hidden_to_y(d).wait_recv()
    for p in range(4):
        rows = slice(p * 256, (p + 1) * 256)
        value = hid_own[y, rows]
        for d in range(3):
            value = value + hid_got[d, rows].astype(F32)
        stack_shifts(value * slope[p], p, adj1, 1, 1, flipped1)
    halo1 = Halo(
        s, c, adj1.at[1, 1:17], adj1.at[4, 1:17], adj1.at[0, 1:17], adj1.at[5, 1:17], h1s, h1r
    )
    halo1.start()

    def first_chunk(j):
        a, b = lax.div(j, 3), lax.rem(j, 3)
        for n in range(2):
            field = u1[pl.ds(a, 4), pl.ds(b, 16), :, n * 256 : (n + 1) * 256].reshape(1024, 256)
            turned = dot(flipped1[...], field).T.astype(BF)
            for k in range(3):
                terms1[3 * j + k, 2 * n : 2 * n + 2] = turned[:, k * 128 : (k + 1) * 128].reshape(2, 4, 32, 128)
        scatter1.start1(j)

    every_chunk(first_chunk)
    halo1.wait_recv()
    for n in range(2):
        value = back_columns(adj1, lambda k: f1[k, 2 * n : 2 * n + 2].reshape(256, 128))
        value = value.reshape(4, 4, 2, 2, 16, 256)
        columns = slice(n * 256, (n + 1) * 256)
        inp_own[:, :, :, :, :, columns] = value
        inp_bf[:, :, :, :, :, columns] = value.astype(BF)
    to_sibling = send(inp_bf.at[:, :, 1 - core], inp_sib, iss.at[0], isr.at[0], sibling)
    to_sibling.start()

    def input_to_y(d):
        n = lax.rem(y + d, 4)
        return send(inp_sum.at[n], inp_got.at[d - 1], iys.at[d - 1], iyr.at[d - 1], (s, n * 2 + core))

    to_sibling.wait_recv()
    for d in (1, 3, 2, 0):
        n = lax.rem(y + d, 4)
        pair = inp_own[:, n, core] + inp_sib[:, n].astype(F32)
        if d:
            inp_sum[n] = pair.astype(BF)
            input_to_y(d).start()
        else:
            grad_in[...] = pair
    every_chunk(scatter2.start2)
    for d in RING:
        input_to_y(d).wait_recv()
    value = grad_in[...]
    for d in range(3):
        value = value + inp_got[d].astype(F32)
    grad_in[...] = value
    every_chunk(scatter1.start2)
    every_chunk(scatter2.finish)
    every_chunk(scatter1.finish)

    halo2.wait_send()
    halo1.wait_send()
    to_sibling.wait_send()
    for n in range(4):
        hidden_to_sibling(n).wait_send()
    for d in RING:
        hidden_to_y(d).wait_send()
        input_to_y(d).wait_send()


def vmem(count):
    return [pl.BlockSpec(memory_space=pltpu.VMEM)] * count


def anywhere(count):
    return [pl.BlockSpec(memory_space=pl.ANY)] * count


def dma(*shape):
    return pltpu.SemaphoreType.DMA(shape)


def local(volume, w_first, b_first, w_second, b_second, cotangent):
    shape = jax.ShapeDtypeStruct
    flops = 2 * 1024 * 27 * 128 * 1536
    features, stacked, flipped, slope, u1, u2, f1, f2 = pl.pallas_call(
        forward_kernel,
        name="forward",
        out_shape=(
            shape((4, 16, 16, 128), BF),
            shape((4, 16, 16, 384), BF),
            shape((384, 1024), BF),
            shape((4, 256, 128), F32),
            shape((6, 18, 16, 512), BF),
            shape((8, 6, 18, 16, 128), BF),
            shape((27, 4, 4, 32, 128), BF),
            shape((27, 4, 4, 64, 128), BF),
        ),
        in_specs=vmem(1) + anywhere(1) + vmem(1) + anywhere(1) + vmem(2),
        out_specs=tuple(vmem(4) + anywhere(4)),
        scratch_shapes=[
            pltpu.VMEM((6, 18, 16, 512), BF),
            pltpu.VMEM((8, 6, 18, 16, 128), BF),
            pltpu.VMEM((27, 4, 4, 32, 128), BF),
            pltpu.VMEM((27, 4, 4, 64, 128), BF),
            pltpu.VMEM((512, 384), F32),
            dma(2, 16), dma(2, 16), dma(2, 16), dma(2, 16),
            dma(2), dma(2), dma(2), dma(2),
            dma(4), dma(4), dma(4), dma(4), dma(4), dma(4), dma(4), dma(4),
            dma(8),
        ],
        compiler_params=pltpu.CompilerParams(
            collective_id=0, has_side_effects=True, vmem_limit_bytes=VMEM_BYTES
        ),
        cost_estimate=pl.CostEstimate(flops=flops, bytes_accessed=40_000_000, transcendentals=600_000),
    )(volume, w_first, b_first.reshape(1, 128), w_second, b_second.reshape(1, 128), cotangent)
    grad_input, grad_first, grad_second = pl.pallas_call(
        backward_kernel,
        name="backward",
        out_shape=(
            shape((4, 2, 16, 512), F32),
            shape((27, 32, 128), F32),
            shape((27, 64, 128), F32),
        ),
        in_specs=vmem(3) + anywhere(1) + vmem(1) + anywhere(2),
        out_specs=tuple(vmem(3)),
        scratch_shapes=[
            pltpu.VMEM((6, 18, 16, 512), BF),
            pltpu.VMEM((27, 4, 4, 32, 128), BF),
            pltpu.VMEM((27, 4, 4, 64, 128), BF),
            pltpu.VMEM((6, 18, 16, 384), BF),
            pltpu.VMEM((6, 18, 16, 384), BF),
            pltpu.VMEM((384, 1024), BF),
            pltpu.VMEM((27, 4, 4, 64, 128), BF),
            pltpu.VMEM((9, 3, 3, 4, 64, 128), BF),
            pltpu.VMEM((9, 3, 4, 64, 128), BF),
            pltpu.VMEM((9, 3, 3, 64, 128), BF),
            pltpu.VMEM((3, 4, 64, 128), F32),
            pltpu.VMEM((27, 4, 4, 32, 128), BF),
            pltpu.VMEM((9, 3, 3, 4, 32, 128), BF),
            pltpu.VMEM((9, 3, 4, 32, 128), BF),
            pltpu.VMEM((9, 3, 3, 32, 128), BF),
            pltpu.VMEM((3, 4, 32, 128), F32),
            pltpu.VMEM((4, 1024, 128), F32),
            pltpu.VMEM((4, 2, 1024, 128), BF),
            pltpu.VMEM((4, 1024, 128), BF),
            pltpu.VMEM((4, 1024, 128), BF),
            pltpu.VMEM((3, 1024, 128), BF),
            pltpu.VMEM((4, 4, 2, 2, 16, 512), F32),
            pltpu.VMEM((4, 4, 2, 2, 16, 512), BF),
            pltpu.VMEM((4, 4, 2, 16, 512), BF),
            pltpu.VMEM((4, 4, 2, 16, 512), BF),
            pltpu.VMEM((3, 4, 2, 16, 512), BF),
            dma(9, 3), dma(9, 3), dma(9, 3), dma(9, 3),
            dma(9, 3), dma(9, 3), dma(9, 3), dma(9, 3),
            dma(2), dma(2), dma(2), dma(2),
            dma(4), dma(4), dma(3), dma(3),
            dma(1), dma(1), dma(3), dma(3),
            dma(4),
        ],
        compiler_params=pltpu.CompilerParams(
            collective_id=1, has_side_effects=True, vmem_limit_bytes=VMEM_BYTES
        ),
        cost_estimate=pl.CostEstimate(flops=2 * flops, bytes_accessed=40_000_000, transcendentals=0),
    )(stacked, flipped, slope, u1, u2, f1, f2)
    return (features, grad_input, grad_first, grad_second)


def solution(mesh):
    return jax.shard_map(
        local,
        mesh=mesh,
        in_specs=(
            P("space", "chan", None, None),
            P(None, "space", "chan"),
            P("chan"),
            P(None, "space", "chan"),
            P("chan"),
            P("space", None, None, "chan"),
        ),
        out_specs=(
            P("space", None, None, "chan"),
            P("space", "chan", None, None),
            P(None, "space", "chan"),
            P(None, "space", "chan"),
        ),
        check_vma=False,
    )
```

```python
import functools

import jax
import jax.numpy as jnp
from jax import lax
from jax.experimental import pallas as pl
from jax.experimental.pallas import tpu as pltpu
from jax.sharding import PartitionSpec as P

MESH = pl.DeviceIdType.MESH
BF = jnp.bfloat16
F32 = jnp.float32
VMEM_BYTES = 63 * 1024 * 1024
RING = (1, 3, 2)
HALVES = ((0, 14), (14, 13))
THIRDS = (((0, 5), (5, 4)), ((9, 4), (13, 5)), ((18, 5), (23, 4)))


def place():
    s = lax.axis_index("space")
    c = lax.axis_index("chan")
    return s, c, lax.div(s, 4), lax.rem(s, 4), lax.div(c, 2), lax.rem(c, 2)


def send(src, dst, send_sem, recv_sem, target):
    return pltpu.make_async_remote_copy(
        src_ref=src,
        dst_ref=dst,
        send_sem=send_sem,
        recv_sem=recv_sem,
        device_id=target,
        device_id_type=MESH,
    )


def greet(s, c, x, z):
    barrier = pltpu.get_barrier_semaphore()

    def signal(space, chan):
        pl.semaphore_signal(barrier, inc=1, device_id=(space, chan), device_id_type=MESH)

    for d in (1, 2, 3):
        signal(lax.rem(x + d, 4) * 4 + z, c)
        signal(x * 4 + lax.rem(z + d, 4), c)
    for d in range(1, 8):
        signal(s, lax.rem(c + d, 8))

    @pl.when(s > 0)
    def _():
        signal(s - 1, c)

    @pl.when(s < 15)
    def _():
        signal(s + 1, c)

    inner = jnp.where(s > 0, 1, 0) + jnp.where(s < 15, 1, 0)
    pl.semaphore_wait(barrier, 13 + inner)


class Halo:
    def __init__(self, s, c, low_src, high_src, low_dst, high_dst, send_sem, recv_sem):
        self.s = s
        self.down = send(low_src, high_dst, send_sem.at[0], recv_sem.at[0], (jnp.maximum(s - 1, 0), c))
        self.up = send(high_src, low_dst, send_sem.at[1], recv_sem.at[1], (jnp.minimum(s + 1, 15), c))

    def start_down(self):
        pl.when(self.s > 0)(self.down.start)

    def start_up(self):
        pl.when(self.s < 15)(self.up.start)

    def start(self):
        self.start_down()
        self.start_up()

    def wait_recv(self):
        pl.when(self.s < 15)(self.down.wait_recv)
        pl.when(self.s > 0)(self.up.wait_recv)

    def wait_send(self):
        pl.when(self.s > 0)(self.down.wait_send)
        pl.when(self.s < 15)(self.up.wait_send)


HOPS = ((1, 0, 0), (3, 0, 0), (1, 1, 1), (3, 3, 2))


class Gather:
    def __init__(self, own, full, x, z, c, send_sem, recv_sem, halves):
        self.own, self.full, self.x, self.z, self.c, self.halves = own, full, x, z, c, halves
        self.send_sem, self.recv_sem = send_sem, recv_sem

    def span(self, half, part):
        k0, nk = self.halves[half]
        cut = (nk + 1) // 2
        return ((k0, nk), (k0, cut), (k0 + cut, nk - cut))[part]

    def region(self, half, first, second, part):
        ox = lax.rem(self.x + 4 - (second if half else first), 4)
        oz = lax.rem(self.z + 4 - (first if half else second), 4)
        k0, nk = self.span(half, part)
        return self.full.at[pl.ds(k0, nk), ox, oz]

    def copy(self, half, row, hop):
        step, behind_by, part = HOPS[hop]
        first, second = (behind_by, 0) if row == 0 else (row - 1, behind_by)
        dst = self.region(half, first, second, part)
        k0, nk = self.span(half, part)
        src = self.own.at[pl.ds(k0, nk)] if first == 0 and second == 0 else dst
        along_x = (row == 0) == (half == 0)
        tx = lax.rem(self.x + step, 4) if along_x else self.x
        tz = self.z if along_x else lax.rem(self.z + step, 4)
        return send(
            src, dst, self.send_sem.at[half, row, hop], self.recv_sem.at[half, row, hop], (tx * 4 + tz, self.c)
        )

    def arrived(self, half, row, hop):
        step, behind_by, part = HOPS[hop]
        distance = (step + behind_by) % 4
        first, second = (distance, 0) if row == 0 else (row - 1, distance)
        region = self.region(half, first, second, part)
        send(
            region,
            region,
            self.send_sem.at[half, row, hop],
            self.recv_sem.at[half, row, hop],
            (lax.rem(self.x + 1, 4) * 4 + self.z, self.c),
        ).wait_recv()

    def start_row(self, half, row):
        self.copy(half, row, 0).start()
        self.copy(half, row, 1).start()

    def start_own(self):
        for row in (0, 1):
            for half in (0, 1):
                self.start_row(half, row)

    def near(self):
        for hop, d in ((0, 1), (1, 3)):
            for half in (0, 1):
                self.arrived(half, 0, hop)
                self.copy(half, 0, hop + 2).start()
                self.start_row(half, 1 + d)

    def relay(self, d):
        for hop in (0, 1):
            for half in (0, 1):
                self.arrived(half, 1 + d, hop)
                self.copy(half, 1 + d, hop + 2).start()

    def far(self):
        for half in (0, 1):
            self.arrived(half, 0, 2)
            self.arrived(half, 0, 3)
            self.start_row(half, 3)

    def finish(self):
        for d in (0, 1, 3, 2):
            for half in (0, 1):
                self.arrived(half, 1 + d, 2)
                self.arrived(half, 1 + d, 3)

    def wait_send(self):
        for half in (0, 1):
            for row in range(5):
                for hop in range(4):
                    self.copy(half, row, hop).wait_send()


class ChanGather:
    def __init__(self, region, s, y, core, y_send, y_recv, c_send, c_recv):
        self.region, self.s, self.y, self.core = region, s, y, core
        self.sems = (y_send, y_recv, c_send, c_recv)

    def to_y(self, d):
        block = self.region(self.y * 2 + self.core)
        y_send, y_recv, _, _ = self.sems
        return send(
            block, block, y_send.at[d], y_recv.at[d], (self.s, lax.rem(self.y + d, 4) * 2 + self.core)
        )

    def from_y(self, d):
        block = self.region(lax.rem(self.y + 4 - d, 4) * 2 + self.core)
        y_send, y_recv, _, _ = self.sems
        return send(
            block, block, y_send.at[d], y_recv.at[d], (self.s, lax.rem(self.y + d, 4) * 2 + self.core)
        )

    def sibling(self, d, other):
        core = (1 - self.core) if other else self.core
        block = self.region(lax.rem(self.y + 4 - d, 4) * 2 + core)
        _, _, c_send, c_recv = self.sems
        return send(block, block, c_send.at[d], c_recv.at[d], (self.s, self.y * 2 + 1 - self.core))

    def start_own(self):
        for d in RING:
            self.to_y(d).start()
        self.sibling(0, False).start()

    def forward(self):
        for d in RING:
            self.from_y(d).wait_recv()
            self.sibling(d, False).start()

    def finish(self):
        for d in range(4):
            self.sibling(d, True).wait_recv()

    def wait_send(self):
        for d in RING:
            self.to_y(d).wait_send()
        for d in range(4):
            self.sibling(d, False).wait_send()


def z_mask(last):
    row = lax.broadcasted_iota(jnp.int32, (256, 128), 0)
    return lax.rem(row, 16) != (15 if last else 0)


def behind(v):
    return jnp.where(z_mask(False), pltpu.roll(v, 1, 0), 0.0)


def ahead(v):
    return jnp.where(z_mask(True), pltpu.roll(v, 255, 0), 0.0)


def slope_of(v):
    sigma = jax.nn.sigmoid(v)
    return sigma * (1.0 + v * (1.0 - sigma))


def stack_shifts(v, xp, stacked, x0, y0, flipped):
    for k, shifted in enumerate((ahead(v), v, behind(v))):
        stacked[xp + x0, y0 : y0 + 16, :, k * 128 : (k + 1) * 128] = shifted.astype(BF).reshape(16, 16, 128)
        flipped[k * 128 : (k + 1) * 128, xp * 256 : (xp + 1) * 256] = shifted.T.astype(BF)


def dot(a, b):
    return jnp.dot(a, b, preferred_element_type=F32)


def convolve_pair(load, load_w, planes, acc):
    def step(j, _):
        a, b = lax.div(j, 3), lax.rem(j, 3)
        rows = jnp.concatenate([load(p + a, b) for p in planes], axis=0)
        filters = jnp.concatenate([load_w(3 * j + k) for k in range(3)], axis=1)
        acc[...] += dot(rows, filters)
        return 0

    acc[...] = jnp.zeros_like(acc)
    lax.fori_loop(0, 9, step, 0)


def convolve_second(field, filters, acc, a):
    def step(b, _):
        rows = jnp.concatenate(
            [field[q, a : a + 4, pl.ds(b, 16)].reshape(1024, 128) for q in range(8)], axis=1
        )
        columns = [filters[9 * a + 3 * b + k].reshape(1024, 128) for k in range(3)]
        acc[...] += dot(rows, jnp.concatenate(columns, axis=1))
        return 0

    lax.fori_loop(0, 3, step, 0)


def plane_of(acc, index):
    rows = slice(index * 256, (index + 1) * 256)
    return behind(acc[rows, 0:128]) + acc[rows, 128:256] + ahead(acc[rows, 256:384])


def forward_kernel(
    vol, w1, b1, w2, b2, cot,
    feat, stacked, flipped, slope, u1_out, u2_out, w1_out, w2_out,
    u1, u2, f1, f2, acc, acc2,
    ag1_s, ag1_r, ag2_s, ag2_r, halo_s, halo_r, hh_s, hh_r, y_s, y_r, c_s, c_r, hy_s, hy_r, hc_s, hc_r, loc,
):
    s, c, x, z, y, core = place()
    u1[0] = jnp.zeros((18, 16, 512), BF)
    u1[5] = jnp.zeros((18, 16, 512), BF)
    for row in (0, 17):
        u1[1:5, row] = jnp.zeros((4, 16, 512), BF)

    def clear(b, _):
        u2[b, 0] = jnp.zeros((18, 16, 128), BF)
        u2[b, 5] = jnp.zeros((18, 16, 128), BF)
        for row in (0, 17):
            u2[b, 1:5, row] = jnp.zeros((4, 16, 128), BF)
        return 0

    lax.fori_loop(0, 8, clear, 0)
    rows_of = lambda cb: u1.at[:, pl.ds(1 + 2 * cb, 2)]
    locals_ = [
        pltpu.make_async_copy(vol, u1.at[1:5, pl.ds(1 + 2 * c, 2)], loc.at[0]),
        pltpu.make_async_copy(w1, f1.at[:, x, z], loc.at[1]),
        pltpu.make_async_copy(w2, f2.at[:, x, z], loc.at[2]),
    ]
    for copy in locals_:
        copy.start()
    greet(s, c, x, z)

    first = Gather(w1, f1, x, z, c, ag1_s, ag1_r, HALVES)
    second = [Gather(w2, f2, x, z, c, ag2_s.at[i], ag2_r.at[i], THIRDS[i]) for i in range(3)]
    halo = Halo(
        s, c, vol.at[0], vol.at[3],
        u1.at[0, pl.ds(1 + 2 * c, 2)], u1.at[5, pl.ds(1 + 2 * c, 2)], halo_s, halo_r,
    )
    rows = ChanGather(rows_of, s, y, core, y_s, y_r, c_s, c_r)
    halo.start()
    first.start_own()
    locals_[0].wait()
    halo.wait_recv()
    rows.start_own()
    first.near()
    first.relay(0)
    first.far()
    rows.forward()
    first.relay(1)
    first.relay(3)
    first.relay(2)
    second[0].start_own()
    second[1].start_own()
    rows.finish()
    locals_[1].wait()
    locals_[2].wait()
    first.finish()
    save_u1 = pltpu.make_async_copy(u1, u1_out, loc.at[3])
    save_w1 = pltpu.make_async_copy(f1, w1_out, loc.at[4])
    save_u1.start()
    save_w1.start()

    hidden_halo = Halo(
        s, c, u2.at[c, 1, 1:17], u2.at[c, 4, 1:17], u2.at[c, 0, 1:17], u2.at[c, 5, 1:17], hh_s, hh_r
    )
    for planes in ((0, 3), (1, 2)):
        convolve_pair(
            lambda p, b: u1[p, pl.ds(b, 16)].reshape(256, 512),
            lambda k: f1[k].reshape(512, 128),
            planes,
            acc,
        )
        for index, p in enumerate(planes):
            pre = plane_of(acc, index) + b1[...]
            slope[p] = slope_of(pre)
            u2[c, p + 1, 1:17] = (pre * jax.nn.sigmoid(pre)).astype(BF).reshape(16, 16, 128)
        if planes == (0, 3):
            hidden_halo.start()
            second[0].near()
    hidden_halo.wait_recv()
    channels = ChanGather(lambda cb: u2.at[cb, :, 1:17], s, y, core, hy_s, hy_r, hc_s, hc_r)
    channels.start_own()
    second[0].relay(0)
    second[0].far()
    second[1].near()
    second[2].start_own()
    second[0].relay(1)
    second[0].relay(3)
    second[0].relay(2)
    second[1].relay(0)
    channels.forward()
    second[1].far()
    second[2].near()
    second[1].relay(1)
    second[1].relay(3)
    channels.finish()
    save_u2 = pltpu.make_async_copy(u2, u2_out, loc.at[5])
    save_u2.start()
    second[1].relay(2)
    second[0].finish()
    acc2[...] = jnp.zeros_like(acc2)
    for a in range(3):
        convolve_second(u2, f2, acc2, a)
        if a == 0:
            second[2].relay(0)
            second[2].far()
            second[2].relay(1)
            second[2].relay(3)
            second[2].relay(2)
        if a < 2:
            second[a + 1].finish()
    save_w2 = pltpu.make_async_copy(f2, w2_out, loc.at[6])
    save_w2.start()
    for p in range(4):
        pre = plane_of(acc2, p) + b2[...]
        feat[p] = (pre * jax.nn.sigmoid(pre)).astype(BF).reshape(16, 16, 128)
        adjoint = cot[p].reshape(256, 128).astype(F32) * slope_of(pre)
        stack_shifts(adjoint, p, stacked, 0, 0, flipped)
    halo.wait_send()
    hidden_halo.wait_send()
    rows.wait_send()
    channels.wait_send()
    first.wait_send()
    for part in second:
        part.wait_send()
    for copy in (save_u1, save_w1, save_u2, save_w2):
        copy.wait()


class Scatter:
    def __init__(self, terms, far1, near1, mid, far2, near2, total, out, x, z, c, sems, flip):
        self.terms, self.far1, self.near1 = terms, far1, near1
        self.mid, self.far2, self.near2 = mid, far2, near2
        self.total, self.out = total, out
        self.x, self.z, self.c, self.flip = x, z, c, flip
        self.s1, self.r1, self.s2, self.r2 = sems
        self.rows = out.shape[1]

    def by_axis(self, j, act):
        x_first = lax.rem(j + self.flip, 2) == 0

        @pl.when(x_first)
        def _():
            act(True)

        @pl.when(jnp.logical_not(x_first))
        def _():
            act(False)

    def target(self, along_x, d):
        tx = lax.rem(self.x + d, 4) if along_x else self.x
        tz = self.z if along_x else lax.rem(self.z + d, 4)
        return tx * 4 + tz, self.c

    def block1(self, j, x_first, d, part=None):
        offsets = pl.ds(3 * j, 3)
        if x_first:
            lead = (offsets, lax.rem(self.x + d, 4))
            return lead if part is None else lead + (slice(2 * part, 2 * part + 2),)
        at = lax.rem(self.z + d, 4)
        return (offsets, slice(None) if part is None else slice(2 * part, 2 * part + 2), at)

    def block2(self, j, x_first, d, part=None):
        at = lax.rem((self.z if x_first else self.x) + d, 4)
        half = self.rows // 2
        lead = (j, slice(None), at)
        return lead if part is None else lead + (slice(half * part, half * (part + 1)),)

    def far(self, stage, j, x_first, way):
        src, dst = (
            (self.terms.at[self.block1(j, x_first, 2, way)], self.far1)
            if stage == 1
            else (self.mid.at[self.block2(j, x_first, 2, way)], self.far2)
        )
        s, r = (self.s1, self.r1) if stage == 1 else (self.s2, self.r2)
        to = self.target(x_first == (stage == 1), (1, 3)[way])
        return send(src, dst.at[j, way], s.at[j, way], r.at[j, way], to)

    def near(self, stage, j, x_first, way):
        step = (1, 3)[way]
        src, dst = (
            (self.terms.at[self.block1(j, x_first, step)], self.near1)
            if stage == 1
            else (self.mid.at[self.block2(j, x_first, step)], self.near2)
        )
        s, r = (self.s1, self.r1) if stage == 1 else (self.s2, self.r2)
        to = self.target(x_first == (stage == 1), step)
        return send(src, dst.at[j, way], s.at[j, 2 + way], r.at[j, 2 + way], to)

    def pass_on(self, stage, j, x_first):
        for way, step in ((0, 1), (1, 3)):
            self.far(stage, j, x_first, way).wait_recv()
            if stage == 1:
                field, got, where = self.terms, self.far1, self.block1(j, x_first, step, way)
            else:
                field, got, where = self.mid, self.far2, self.block2(j, x_first, step, way)
            field[where] = (field[where].astype(F32) + got[j, way].astype(F32)).astype(BF)
            self.near(stage, j, x_first, way).start()

    def start1(self, j):
        def act(x_first):
            self.far(1, j, x_first, 0).start()
            self.far(1, j, x_first, 1).start()

        self.by_axis(j, act)

    def relay1(self, j):
        self.by_axis(j, lambda x_first: self.pass_on(1, j, x_first))

    def start2(self, j):
        def act(x_first):
            value = self.terms[self.block1(j, x_first, 0)].astype(F32)
            for way in (0, 1):
                self.near(1, j, x_first, way).wait_recv()
                value = value + self.near1[j, way].astype(F32)
            self.total[...] = value
            self.mid[j] = value.astype(BF)
            self.far(2, j, x_first, 0).start()
            self.far(2, j, x_first, 1).start()
            self.out[pl.ds(3 * j, 3)] = self.total[:, self.z] if x_first else self.total[:, self.x]

        self.by_axis(j, act)

    def relay2(self, j):
        self.by_axis(j, lambda x_first: self.pass_on(2, j, x_first))

    def finish(self, j):
        def act(x_first):
            value = self.out[pl.ds(3 * j, 3)]
            for way in (0, 1):
                self.near(2, j, x_first, way).wait_recv()
                value = value + self.near2[j, way].astype(F32)
            self.out[pl.ds(3 * j, 3)] = value
            for stage in (1, 2):
                for way in (0, 1):
                    self.far(stage, j, x_first, way).wait_send()
                    self.near(stage, j, x_first, way).wait_send()

        self.by_axis(j, act)


def every_chunk(act, start=0, stop=9):
    def step(j, _):
        act(j)
        return 0

    lax.fori_loop(start, stop, step, 0)


def back_columns(stacked, load_w):
    total = None
    for a in range(3):
        rows = jnp.concatenate(
            [stacked[2 - a : 6 - a, 2 - b : 18 - b].reshape(1024, 384) for b in range(3)], axis=1
        )
        filters = jnp.concatenate([load_w(9 * a + k) for k in range(9)], axis=1)
        term = lax.dot_general(rows, filters, (((1,), (1,)), ((), ())), preferred_element_type=F32)
        total = term if total is None else total + term
    return total


def backward_kernel(
    stacked_in, flipped2, slope, u1_in, u2, w1_in, w2_in,
    grad_in, grad1, grad2,
    u1, f1, f2, adj2, adj1, flipped1,
    terms2, far2a, near2a, mid2, far2b, near2b, total2,
    terms1, far1a, near1a, mid1, far1b, near1b, total1,
    hid_own, hid_bf, hid_sib, hid_sum, hid_got,
    inp_own, inp_bf, inp_sib, inp_sum, inp_got,
    g2s1, g2r1, g2s2, g2r2, g1s1, g1r1, g1s2, g1r2,
    h2s, h2r, h1s, h1r, hss, hsr, hys, hyr, iss, isr, iys, iyr, loc,
):
    s, c, x, z, y, core = place()
    loads = [
        pltpu.make_async_copy(stacked_in, adj2.at[1:5, 1:17], loc.at[0]),
        pltpu.make_async_copy(w2_in, f2, loc.at[1]),
        pltpu.make_async_copy(u1_in, u1, loc.at[2]),
        pltpu.make_async_copy(w1_in, f1, loc.at[3]),
    ]
    for copy in loads:
        copy.start()
    for field in (adj2, adj1):
        for plane in (0, 5):
            field[plane] = jnp.zeros((18, 16, 384), BF)
        for row in (0, 17):
            field[1:5, row] = jnp.zeros((4, 16, 384), BF)
    greet(s, c, x, z)
    sibling = (s, y * 2 + 1 - core)

    halo2 = Halo(
        s, c, stacked_in.at[0], stacked_in.at[3], adj2.at[0, 1:17], adj2.at[5, 1:17], h2s, h2r
    )
    halo2.start()
    scatter2 = Scatter(
        terms2, far2a, near2a, mid2, far2b, near2b, total2, grad2, x, z, c, (g2s1, g2r1, g2s2, g2r2), 0
    )
    scatter1 = Scatter(
        terms1, far1a, near1a, mid1, far1b, near1b, total1, grad1, x, z, c, (g1s1, g1r1, g1s2, g1r2), 1
    )

    def second_chunk(j):
        a, b = lax.div(j, 3), lax.rem(j, 3)

        def block(n, _):
            fields = [u2[2 * n + q, pl.ds(a, 4), pl.ds(b, 16)].reshape(1024, 128) for q in range(2)]
            turned = dot(flipped2[...], jnp.concatenate(fields, axis=1)).T.astype(BF)
            for k in range(3):
                terms2[3 * j + k, n] = turned[:, k * 128 : (k + 1) * 128].reshape(4, 64, 128)
            return 0

        lax.fori_loop(0, 4, block, 0)
        scatter2.start1(j)

    every_chunk(second_chunk, 0, 4)
    for copy in loads:
        copy.wait()
    halo2.wait_recv()

    def hidden_to_sibling(n):
        return send(hid_bf.at[n, 1 - core], hid_sib.at[n], hss.at[n], hsr.at[n], sibling)

    def hidden_columns(n, _):
        value = back_columns(adj2, lambda k: f2[k, n].reshape(256, 128))
        low, high = value[:, :128], value[:, 128:]
        hid_bf[n, 0] = low.astype(BF)
        hid_bf[n, 1] = high.astype(BF)
        hid_own[n] = jnp.where(core == 0, low, high)
        hidden_to_sibling(n).start()
        scatter2.relay1(n)
        return 0

    lax.fori_loop(0, 4, hidden_columns, 0)

    def hidden_to_y(d):
        n = lax.rem(y + d, 4)
        return send(hid_sum.at[n], hid_got.at[d - 1], hys.at[d - 1], hyr.at[d - 1], (s, n * 2 + core))

    for d in (1, 3, 2, 0):
        n = lax.rem(y + d, 4)
        hidden_to_sibling(n).wait_recv()
        pair = hid_own[n] + hid_sib[n].astype(F32)
        if d:
            hid_sum[n] = pair.astype(BF)
            hidden_to_y(d).start()
        else:
            hid_own[n] = pair

    def late_chunk(j):
        second_chunk(j)
        pl.when(j < 8)(lambda: scatter2.start2(jnp.maximum(j - 4, 0)))
        pl.when(j >= 6)(lambda: scatter2.relay1(jnp.maximum(j - 2, 0)))

    every_chunk(late_chunk, 4, 9)
    for d in RING:
        hidden_to_y(d).wait_recv()
    for p in range(4):
        rows = slice(p * 256, (p + 1) * 256)
        value = hid_own[y, rows]
        for d in range(3):
            value = value + hid_got[d, rows].astype(F32)
        stack_shifts(value * slope[p], p, adj1, 1, 1, flipped1)
    halo1 = Halo(
        s, c, adj1.at[1, 1:17], adj1.at[4, 1:17], adj1.at[0, 1:17], adj1.at[5, 1:17], h1s, h1r
    )
    halo1.start()

    def first_chunk(j):
        a, b = lax.div(j, 3), lax.rem(j, 3)
        for n in range(2):
            field = u1[pl.ds(a, 4), pl.ds(b, 16), :, n * 256 : (n + 1) * 256].reshape(1024, 256)
            turned = dot(flipped1[...], field).T.astype(BF)
            for k in range(3):
                terms1[3 * j + k, 2 * n : 2 * n + 2] = turned[:, k * 128 : (k + 1) * 128].reshape(2, 4, 32, 128)
        scatter1.start1(j)

    every_chunk(first_chunk, 0, 3)
    scatter2.relay1(7)
    every_chunk(first_chunk, 3, 6)
    scatter2.relay1(8)
    every_chunk(first_chunk, 6, 9)
    every_chunk(scatter1.relay1, 0, 3)
    every_chunk(scatter2.relay2, 0, 4)
    halo1.wait_recv()
    for n in range(2):
        value = back_columns(adj1, lambda k: f1[k, 2 * n : 2 * n + 2].reshape(256, 128))
        value = value.reshape(4, 4, 2, 2, 16, 256)
        columns = slice(n * 256, (n + 1) * 256)
        inp_own[:, :, :, :, :, columns] = value
        inp_bf[:, :, :, :, :, columns] = value.astype(BF)
        if n == 0:
            every_chunk(scatter1.relay1, 3, 6)
            every_chunk(scatter2.start2, 4, 6)
    to_sibling = send(inp_bf.at[:, :, 1 - core], inp_sib, iss.at[0], isr.at[0], sibling)
    to_sibling.start()

    def input_to_y(d):
        n = lax.rem(y + d, 4)
        return send(inp_sum.at[n], inp_got.at[d - 1], iys.at[d - 1], iyr.at[d - 1], (s, n * 2 + core))

    every_chunk(scatter1.relay1, 6, 9)
    to_sibling.wait_recv()
    for d in (1, 3, 2, 0):
        n = lax.rem(y + d, 4)
        pair = inp_own[:, n, core] + inp_sib[:, n].astype(F32)
        if d:
            inp_sum[n] = pair.astype(BF)
            input_to_y(d).start()
        else:
            grad_in[...] = pair
    every_chunk(scatter2.start2, 6, 9)
    every_chunk(scatter1.start2, 0, 4)
    every_chunk(scatter2.relay2, 4, 9)
    every_chunk(scatter1.start2, 4, 9)
    for d in RING:
        input_to_y(d).wait_recv()
    value = grad_in[...]
    for d in range(3):
        value = value + inp_got[d].astype(F32)
    grad_in[...] = value
    every_chunk(scatter2.finish)
    every_chunk(scatter1.relay2)
    every_chunk(scatter1.finish)

    halo2.wait_send()
    halo1.wait_send()
    to_sibling.wait_send()
    for n in range(4):
        hidden_to_sibling(n).wait_send()
    for d in RING:
        hidden_to_y(d).wait_send()
        input_to_y(d).wait_send()


def hand_over(*refs):
    for i in range(4):
        refs[4 + i][...] = refs[i][...]


def vmem(count):
    return [pl.BlockSpec(memory_space=pltpu.VMEM)] * count


def anywhere(count):
    return [pl.BlockSpec(memory_space=pl.ANY)] * count


def dma(*shape):
    return pltpu.SemaphoreType.DMA(shape)


def local(volume, w_first, b_first, w_second, b_second, cotangent):
    shape = jax.ShapeDtypeStruct
    flops = 2 * 1024 * 27 * 128 * 1536
    features, stacked, flipped, slope, u1, u2, f1, f2 = pl.pallas_call(
        forward_kernel,
        name="forward",
        out_shape=(
            shape((4, 16, 16, 128), BF),
            shape((4, 16, 16, 384), BF),
            shape((384, 1024), BF),
            shape((4, 256, 128), F32),
            shape((6, 18, 16, 512), BF),
            shape((8, 6, 18, 16, 128), BF),
            shape((27, 4, 4, 32, 128), BF),
            shape((27, 4, 4, 64, 128), BF),
        ),
        in_specs=vmem(1) + anywhere(1) + vmem(1) + anywhere(1) + vmem(2),
        out_specs=tuple(vmem(4) + anywhere(4)),
        scratch_shapes=[
            pltpu.VMEM((6, 18, 16, 512), BF),
            pltpu.VMEM((8, 6, 18, 16, 128), BF),
            pltpu.VMEM((27, 4, 4, 32, 128), BF),
            pltpu.VMEM((27, 4, 4, 64, 128), BF),
            pltpu.VMEM((512, 384), F32),
            pltpu.VMEM((1024, 384), F32),
            dma(2, 5, 4), dma(2, 5, 4), dma(3, 2, 5, 4), dma(3, 2, 5, 4),
            dma(2), dma(2), dma(2), dma(2),
            dma(4), dma(4), dma(4), dma(4), dma(4), dma(4), dma(4), dma(4),
            dma(8),
        ],
        compiler_params=pltpu.CompilerParams(
            collective_id=0, has_side_effects=True, vmem_limit_bytes=VMEM_BYTES
        ),
        cost_estimate=pl.CostEstimate(flops=flops, bytes_accessed=40_000_000, transcendentals=600_000),
    )(volume, w_first, b_first.reshape(1, 128), w_second, b_second.reshape(1, 128), cotangent)
    grad_input, grad_first, grad_second = pl.pallas_call(
        backward_kernel,
        name="backward",
        out_shape=(
            shape((4, 2, 16, 512), F32),
            shape((27, 32, 128), F32),
            shape((27, 64, 128), F32),
        ),
        in_specs=vmem(3) + anywhere(1) + vmem(1) + anywhere(2),
        out_specs=tuple(vmem(3)),
        scratch_shapes=[
            pltpu.VMEM((6, 18, 16, 512), BF),
            pltpu.VMEM((27, 4, 4, 32, 128), BF),
            pltpu.VMEM((27, 4, 4, 64, 128), BF),
            pltpu.VMEM((6, 18, 16, 384), BF),
            pltpu.VMEM((6, 18, 16, 384), BF),
            pltpu.VMEM((384, 1024), BF),
            pltpu.VMEM((27, 4, 4, 64, 128), BF),
            pltpu.VMEM((9, 2, 3, 2, 64, 128), BF),
            pltpu.VMEM((9, 2, 3, 4, 64, 128), BF),
            pltpu.VMEM((9, 3, 4, 64, 128), BF),
            pltpu.VMEM((9, 2, 3, 32, 128), BF),
            pltpu.VMEM((9, 2, 3, 64, 128), BF),
            pltpu.VMEM((3, 4, 64, 128), F32),
            pltpu.VMEM((27, 4, 4, 32, 128), BF),
            pltpu.VMEM((9, 2, 3, 2, 32, 128), BF),
            pltpu.VMEM((9, 2, 3, 4, 32, 128), BF),
            pltpu.VMEM((9, 3, 4, 32, 128), BF),
            pltpu.VMEM((9, 2, 3, 16, 128), BF),
            pltpu.VMEM((9, 2, 3, 32, 128), BF),
            pltpu.VMEM((3, 4, 32, 128), F32),
            pltpu.VMEM((4, 1024, 128), F32),
            pltpu.VMEM((4, 2, 1024, 128), BF),
            pltpu.VMEM((4, 1024, 128), BF),
            pltpu.VMEM((4, 1024, 128), BF),
            pltpu.VMEM((3, 1024, 128), BF),
            pltpu.VMEM((4, 4, 2, 2, 16, 512), F32),
            pltpu.VMEM((4, 4, 2, 2, 16, 512), BF),
            pltpu.VMEM((4, 4, 2, 16, 512), BF),
            pltpu.VMEM((4, 4, 2, 16, 512), BF),
            pltpu.VMEM((3, 4, 2, 16, 512), BF),
            dma(9, 4), dma(9, 4), dma(9, 4), dma(9, 4),
            dma(9, 4), dma(9, 4), dma(9, 4), dma(9, 4),
            dma(2), dma(2), dma(2), dma(2),
            dma(4), dma(4), dma(3), dma(3),
            dma(1), dma(1), dma(3), dma(3),
            dma(4),
        ],
        compiler_params=pltpu.CompilerParams(
            collective_id=1, has_side_effects=True, vmem_limit_bytes=VMEM_BYTES
        ),
        cost_estimate=pl.CostEstimate(flops=2 * flops, bytes_accessed=40_000_000, transcendentals=0),
    )(stacked, flipped, slope, u1, u2, f1, f2)
    results = (features, grad_input, grad_first, grad_second)
    return pl.pallas_call(
        hand_over,
        name="hand_over",
        out_shape=tuple(shape(r.shape, r.dtype) for r in results),
        in_specs=vmem(4),
        out_specs=tuple(vmem(4)),
        compiler_params=pltpu.CompilerParams(vmem_limit_bytes=VMEM_BYTES),
    )(*results)


def solution(mesh):
    return jax.shard_map(
        local,
        mesh=mesh,
        in_specs=(
            P("space", "chan", None, None),
            P(None, "space", "chan"),
            P("chan"),
            P(None, "space", "chan"),
            P("chan"),
            P("space", None, None, "chan"),
        ),
        out_specs=(
            P("space", None, None, "chan"),
            P("space", "chan", None, None),
            P(None, "space", "chan"),
            P(None, "space", "chan"),
        ),
        check_vma=False,
    )
```

```python
import functools

import jax
import jax.numpy as jnp
from jax import lax
from jax.experimental import pallas as pl
from jax.experimental.pallas import tpu as pltpu
from jax.sharding import PartitionSpec as P

MESH = pl.DeviceIdType.MESH
BF = jnp.bfloat16
F32 = jnp.float32
VMEM_BYTES = 63 * 1024 * 1024
RING = (1, 3, 2)
HALVES = ((0, 14), (14, 13))
THIRDS = (((0, 5), (5, 4)), ((9, 4), (13, 5)), ((18, 5), (23, 4)))


def place():
    s = lax.axis_index("space")
    c = lax.axis_index("chan")
    return s, c, lax.div(s, 4), lax.rem(s, 4), lax.div(c, 2), lax.rem(c, 2)


def send(src, dst, send_sem, recv_sem, target):
    return pltpu.make_async_remote_copy(
        src_ref=src,
        dst_ref=dst,
        send_sem=send_sem,
        recv_sem=recv_sem,
        device_id=target,
        device_id_type=MESH,
    )


def greet(s, c, x, z):
    barrier = pltpu.get_barrier_semaphore()

    def signal(space, chan):
        pl.semaphore_signal(barrier, inc=1, device_id=(space, chan), device_id_type=MESH)

    for d in (1, 2, 3):
        signal(lax.rem(x + d, 4) * 4 + z, c)
        signal(x * 4 + lax.rem(z + d, 4), c)
    for d in range(1, 8):
        signal(s, lax.rem(c + d, 8))

    @pl.when(s > 0)
    def _():
        signal(s - 1, c)

    @pl.when(s < 15)
    def _():
        signal(s + 1, c)

    inner = jnp.where(s > 0, 1, 0) + jnp.where(s < 15, 1, 0)
    pl.semaphore_wait(barrier, 13 + inner)


class Halo:
    def __init__(self, s, c, low_src, high_src, low_dst, high_dst, send_sem, recv_sem):
        self.s = s
        self.down = send(low_src, high_dst, send_sem.at[0], recv_sem.at[0], (jnp.maximum(s - 1, 0), c))
        self.up = send(high_src, low_dst, send_sem.at[1], recv_sem.at[1], (jnp.minimum(s + 1, 15), c))

    def start_down(self):
        pl.when(self.s > 0)(self.down.start)

    def start_up(self):
        pl.when(self.s < 15)(self.up.start)

    def start(self):
        self.start_down()
        self.start_up()

    def wait_recv(self):
        pl.when(self.s < 15)(self.down.wait_recv)
        pl.when(self.s > 0)(self.up.wait_recv)

    def wait_send(self):
        pl.when(self.s > 0)(self.down.wait_send)
        pl.when(self.s < 15)(self.up.wait_send)


HOPS = ((1, 0, 0), (3, 0, 0), (1, 1, 1), (3, 3, 2))


class Gather:
    def __init__(self, own, full, x, z, c, send_sem, recv_sem, halves):
        self.own, self.full, self.x, self.z, self.c, self.halves = own, full, x, z, c, halves
        self.send_sem, self.recv_sem = send_sem, recv_sem

    def span(self, half, part):
        k0, nk = self.halves[half]
        cut = (nk + 1) // 2
        return ((k0, nk), (k0, cut), (k0 + cut, nk - cut))[part]

    def region(self, half, first, second, part):
        ox = lax.rem(self.x + 4 - (second if half else first), 4)
        oz = lax.rem(self.z + 4 - (first if half else second), 4)
        k0, nk = self.span(half, part)
        return self.full.at[pl.ds(k0, nk), ox, oz]

    def copy(self, half, row, hop):
        step, behind_by, part = HOPS[hop]
        first, second = (behind_by, 0) if row == 0 else (row - 1, behind_by)
        dst = self.region(half, first, second, part)
        k0, nk = self.span(half, part)
        src = self.own.at[pl.ds(k0, nk)] if first == 0 and second == 0 else dst
        along_x = (row == 0) == (half == 0)
        tx = lax.rem(self.x + step, 4) if along_x else self.x
        tz = self.z if along_x else lax.rem(self.z + step, 4)
        return send(
            src, dst, self.send_sem.at[half, row, hop], self.recv_sem.at[half, row, hop], (tx * 4 + tz, self.c)
        )

    def arrived(self, half, row, hop):
        step, behind_by, part = HOPS[hop]
        distance = (step + behind_by) % 4
        first, second = (distance, 0) if row == 0 else (row - 1, distance)
        region = self.region(half, first, second, part)
        send(
            region,
            region,
            self.send_sem.at[half, row, hop],
            self.recv_sem.at[half, row, hop],
            (lax.rem(self.x + 1, 4) * 4 + self.z, self.c),
        ).wait_recv()

    def start_row(self, half, row):
        self.copy(half, row, 0).start()
        self.copy(half, row, 1).start()

    def start_own(self):
        for row in (0, 1):
            for half in (0, 1):
                self.start_row(half, row)

    def near(self):
        for hop, d in ((0, 1), (1, 3)):
            for half in (0, 1):
                self.arrived(half, 0, hop)
                self.copy(half, 0, hop + 2).start()
                self.start_row(half, 1 + d)

    def relay(self, d):
        for hop in (0, 1):
            for half in (0, 1):
                self.arrived(half, 1 + d, hop)
                self.copy(half, 1 + d, hop + 2).start()

    def far(self):
        for half in (0, 1):
            self.arrived(half, 0, 2)
            self.arrived(half, 0, 3)
            self.start_row(half, 3)

    def finish(self):
        for d in (0, 1, 3, 2):
            for half in (0, 1):
                self.arrived(half, 1 + d, 2)
                self.arrived(half, 1 + d, 3)

    def wait_send(self):
        for half in (0, 1):
            for row in range(5):
                for hop in range(4):
                    self.copy(half, row, hop).wait_send()


class ChanGather:
    def __init__(self, region, s, y, core, y_send, y_recv, c_send, c_recv):
        self.region, self.s, self.y, self.core = region, s, y, core
        self.sems = (y_send, y_recv, c_send, c_recv)

    def to_y(self, d):
        block = self.region(self.y * 2 + self.core)
        y_send, y_recv, _, _ = self.sems
        return send(
            block, block, y_send.at[d], y_recv.at[d], (self.s, lax.rem(self.y + d, 4) * 2 + self.core)
        )

    def from_y(self, d):
        block = self.region(lax.rem(self.y + 4 - d, 4) * 2 + self.core)
        y_send, y_recv, _, _ = self.sems
        return send(
            block, block, y_send.at[d], y_recv.at[d], (self.s, lax.rem(self.y + d, 4) * 2 + self.core)
        )

    def sibling(self, d, other):
        core = (1 - self.core) if other else self.core
        block = self.region(lax.rem(self.y + 4 - d, 4) * 2 + core)
        _, _, c_send, c_recv = self.sems
        return send(block, block, c_send.at[d], c_recv.at[d], (self.s, self.y * 2 + 1 - self.core))

    def start_own(self):
        for d in RING:
            self.to_y(d).start()
        self.sibling(0, False).start()

    def forward(self):
        for d in RING:
            self.from_y(d).wait_recv()
            self.sibling(d, False).start()

    def finish(self):
        for d in range(4):
            self.sibling(d, True).wait_recv()

    def wait_send(self):
        for d in RING:
            self.to_y(d).wait_send()
        for d in range(4):
            self.sibling(d, False).wait_send()


def z_mask(last):
    row = lax.broadcasted_iota(jnp.int32, (256, 128), 0)
    return lax.rem(row, 16) != (15 if last else 0)


def behind(v):
    return jnp.where(z_mask(False), pltpu.roll(v, 1, 0), 0.0)


def ahead(v):
    return jnp.where(z_mask(True), pltpu.roll(v, 255, 0), 0.0)


def slope_of(v):
    sigma = jax.nn.sigmoid(v)
    return sigma * (1.0 + v * (1.0 - sigma))


def stack_shifts(v, xp, stacked, x0, y0, flipped=None):
    for k, shifted in enumerate((ahead(v), v, behind(v))):
        stacked[xp + x0, y0 : y0 + 16, :, k * 128 : (k + 1) * 128] = shifted.astype(BF).reshape(16, 16, 128)
        if flipped is not None:
            flipped[k * 128 : (k + 1) * 128, xp * 256 : (xp + 1) * 256] = shifted.T.astype(BF)


def dot(a, b):
    return jnp.dot(a, b, preferred_element_type=F32)


def convolve_part(load, load_w, a, acc):
    rows = jnp.concatenate([load(a, b) for b in range(3)], axis=1)
    filters = jnp.concatenate(
        [jnp.concatenate([load_w(9 * a + 3 * b + k) for k in range(3)], axis=1) for b in range(3)], axis=0
    )
    acc[...] += dot(rows, filters)


def plane_of(acc, index):
    rows = slice(index * 256, (index + 1) * 256)
    return behind(acc[rows, 0:128]) + acc[rows, 128:256] + ahead(acc[rows, 256:384])


def forward_kernel(
    vol, w1, b1, w2, b2, cot,
    feat, stacked, flipped, slope, u1_out, u2_out, w1_out, w2_out,
    u1, u2, f1, f2, acc,
    ag1_s, ag1_r, ag2_s, ag2_r, halo_s, halo_r, hh_s, hh_r, y_s, y_r, c_s, c_r, hy_s, hy_r, hc_s, hc_r, loc,
):
    s, c, x, z, y, core = place()
    u1[0] = jnp.zeros((18, 16, 512), BF)
    u1[5] = jnp.zeros((18, 16, 512), BF)
    for row in (0, 17):
        u1[1:5, row] = jnp.zeros((4, 16, 512), BF)

    def clear(b, _):
        u2[b, 0] = jnp.zeros((18, 16, 128), BF)
        u2[b, 5] = jnp.zeros((18, 16, 128), BF)
        for row in (0, 17):
            u2[b, 1:5, row] = jnp.zeros((4, 16, 128), BF)
        return 0

    lax.fori_loop(0, 8, clear, 0)
    rows_of = lambda cb: u1.at[:, pl.ds(1 + 2 * cb, 2)]
    locals_ = [
        pltpu.make_async_copy(vol, u1.at[1:5, pl.ds(1 + 2 * c, 2)], loc.at[0]),
        pltpu.make_async_copy(w1, f1.at[:, x, z], loc.at[1]),
        pltpu.make_async_copy(w2, f2.at[:, x, z], loc.at[2]),
    ]
    for copy in locals_:
        copy.start()
    greet(s, c, x, z)

    first = Gather(w1, f1, x, z, c, ag1_s, ag1_r, HALVES)
    second = [Gather(w2, f2, x, z, c, ag2_s.at[i], ag2_r.at[i], THIRDS[i]) for i in range(3)]
    halo = Halo(
        s, c, vol.at[0], vol.at[3],
        u1.at[0, pl.ds(1 + 2 * c, 2)], u1.at[5, pl.ds(1 + 2 * c, 2)], halo_s, halo_r,
    )
    rows = ChanGather(rows_of, s, y, core, y_s, y_r, c_s, c_r)
    halo.start()
    first.start_own()
    locals_[0].wait()
    halo.wait_recv()
    first.near()
    rows.start_own()
    first.relay(0)
    first.far()
    first.relay(1)
    first.relay(3)
    rows.forward()
    first.relay(2)
    rows.finish()
    second[0].start_own()
    second[1].start_own()
    locals_[1].wait()
    locals_[2].wait()
    acc[...] = jnp.zeros_like(acc)
    first.finish()
    save_u1 = pltpu.make_async_copy(u1, u1_out, loc.at[3])
    save_w1 = pltpu.make_async_copy(f1, w1_out, loc.at[4])
    save_u1.start()
    save_w1.start()

    hidden_halo = Halo(
        s, c, u2.at[c, 1, 1:17], u2.at[c, 4, 1:17], u2.at[c, 0, 1:17], u2.at[c, 5, 1:17], hh_s, hh_r
    )
    for a in range(3):
        convolve_part(
            lambda a, b: u1[a : a + 4, b : b + 16].reshape(1024, 512),
            lambda k: f1[k].reshape(512, 128),
            a,
            acc,
        )
        if a == 0:
            second[0].near()
    for p in (0, 3, 1, 2):
        pre = plane_of(acc, p) + b1[...]
        slope[p] = slope_of(pre)
        u2[c, p + 1, 1:17] = (pre * jax.nn.sigmoid(pre)).astype(BF).reshape(16, 16, 128)
        if p == 3:
            hidden_halo.start()
            second[2].start_own()
    channels, low_rim, high_rim = [
        ChanGather(
            lambda cb, planes=planes: u2.at[cb, planes, 1:17],
            s, y, core, hy_s.at[i], hy_r.at[i], hc_s.at[i], hc_r.at[i],
        )
        for i, planes in enumerate((slice(1, 5), 0, 5))
    ]
    channels.start_own()
    second[0].relay(3)
    second[1].near()
    acc[...] = jnp.zeros_like(acc)
    second[2].near()
    hidden_halo.wait_recv()
    low_rim.start_own()
    high_rim.start_own()
    second[0].far()
    second[0].relay(0)
    second[1].far()
    channels.forward()
    second[0].relay(1)
    second[1].relay(0)
    second[0].relay(2)
    second[1].relay(3)
    low_rim.forward()
    high_rim.forward()
    second[1].relay(1)
    second[2].far()
    channels.finish()
    low_rim.finish()
    high_rim.finish()
    save_u2 = pltpu.make_async_copy(u2, u2_out, loc.at[5])
    save_u2.start()
    second[1].relay(2)
    second[2].relay(3)
    second[2].relay(1)
    second[0].finish()
    second[2].relay(0)
    for a in range(3):
        convolve_part(
            lambda a, b: jnp.concatenate(
                [u2[q, a : a + 4, b : b + 16].reshape(1024, 128) for q in range(8)], axis=1
            ),
            lambda k: f2[k].reshape(1024, 128),
            a,
            acc,
        )
        if a < 2:
            second[a + 1].finish()
        if a == 0:
            second[2].relay(2)
    save_w2 = pltpu.make_async_copy(f2, w2_out, loc.at[6])
    save_w2.start()
    for p in range(4):
        pre = plane_of(acc, p) + b2[...]
        feat[p] = (pre * jax.nn.sigmoid(pre)).astype(BF).reshape(16, 16, 128)
        adjoint = cot[p].reshape(256, 128).astype(F32) * slope_of(pre)
        stack_shifts(adjoint, p, stacked, 0, 0, flipped)
    halo.wait_send()
    hidden_halo.wait_send()
    rows.wait_send()
    for part in (channels, low_rim, high_rim):
        part.wait_send()
    first.wait_send()
    for part in second:
        part.wait_send()
    for copy in (save_u1, save_w1, save_u2, save_w2):
        copy.wait()


class Scatter:
    def __init__(self, terms, far1, near1, mid, far2, near2, total, out, x, z, c, sems, flip):
        self.terms, self.far1, self.near1 = terms, far1, near1
        self.mid, self.far2, self.near2 = mid, far2, near2
        self.total, self.out = total, out
        self.x, self.z, self.c, self.flip = x, z, c, flip
        self.s1, self.r1, self.s2, self.r2 = sems
        self.rows = out.shape[1]

    def by_axis(self, j, act):
        if isinstance(j, int):
            return act((j + self.flip) % 2 == 0)
        x_first = lax.rem(j + self.flip, 2) == 0

        @pl.when(x_first)
        def _():
            act(True)

        @pl.when(jnp.logical_not(x_first))
        def _():
            act(False)

    def target(self, along_x, d):
        tx = lax.rem(self.x + d, 4) if along_x else self.x
        tz = self.z if along_x else lax.rem(self.z + d, 4)
        return tx * 4 + tz, self.c

    def block1(self, j, x_first, d, part=None):
        offsets = pl.ds(3 * j, 3)
        if x_first:
            lead = (offsets, lax.rem(self.x + d, 4))
            return lead if part is None else lead + (slice(2 * part, 2 * part + 2),)
        at = lax.rem(self.z + d, 4)
        return (offsets, slice(None) if part is None else slice(2 * part, 2 * part + 2), at)

    def block2(self, j, x_first, d, part=None):
        at = lax.rem((self.z if x_first else self.x) + d, 4)
        half = self.rows // 2
        lead = (j, slice(None), at)
        return lead if part is None else lead + (slice(half * part, half * (part + 1)),)

    def far(self, stage, j, x_first, way):
        src, dst = (
            (self.terms.at[self.block1(j, x_first, 2, way)], self.far1)
            if stage == 1
            else (self.mid.at[self.block2(j, x_first, 2, way)], self.far2)
        )
        s, r = (self.s1, self.r1) if stage == 1 else (self.s2, self.r2)
        to = self.target(x_first == (stage == 1), (1, 3)[way])
        return send(src, dst.at[j, way], s.at[j, way], r.at[j, way], to)

    def near(self, stage, j, x_first, way):
        step = (1, 3)[way]
        src, dst = (
            (self.terms.at[self.block1(j, x_first, step)], self.near1)
            if stage == 1
            else (self.mid.at[self.block2(j, x_first, step)], self.near2)
        )
        s, r = (self.s1, self.r1) if stage == 1 else (self.s2, self.r2)
        to = self.target(x_first == (stage == 1), step)
        return send(src, dst.at[j, way], s.at[j, 2 + way], r.at[j, 2 + way], to)

    def pass_on(self, stage, j, x_first):
        for way, step in ((0, 1), (1, 3)):
            self.far(stage, j, x_first, way).wait_recv()
            if stage == 1:
                field, got, where = self.terms, self.far1, self.block1(j, x_first, step, way)
            else:
                field, got, where = self.mid, self.far2, self.block2(j, x_first, step, way)
            field[where] = (field[where].astype(F32) + got[j, way].astype(F32)).astype(BF)
            self.near(stage, j, x_first, way).start()

    def start1(self, j):
        def act(x_first):
            self.far(1, j, x_first, 0).start()
            self.far(1, j, x_first, 1).start()

        self.by_axis(j, act)

    def relay1(self, j):
        self.by_axis(j, lambda x_first: self.pass_on(1, j, x_first))

    def start2(self, j):
        def act(x_first):
            value = self.terms[self.block1(j, x_first, 0)].astype(F32)
            for way in (0, 1):
                self.near(1, j, x_first, way).wait_recv()
                value = value + self.near1[j, way].astype(F32)
            self.total[...] = value
            self.mid[j] = value.astype(BF)
            self.far(2, j, x_first, 0).start()
            self.far(2, j, x_first, 1).start()
            self.out[pl.ds(3 * j, 3)] = self.total[:, self.z] if x_first else self.total[:, self.x]

        self.by_axis(j, act)

    def relay2(self, j):
        self.by_axis(j, lambda x_first: self.pass_on(2, j, x_first))

    def finish(self, j):
        def act(x_first):
            value = self.out[pl.ds(3 * j, 3)]
            for way in (0, 1):
                self.near(2, j, x_first, way).wait_recv()
                value = value + self.near2[j, way].astype(F32)
            self.out[pl.ds(3 * j, 3)] = value
            for stage in (1, 2):
                for way in (0, 1):
                    self.far(stage, j, x_first, way).wait_send()
                    self.near(stage, j, x_first, way).wait_send()

        self.by_axis(j, act)


def every_chunk(act, start=0, stop=9):
    def step(j, _):
        act(j)
        return 0

    lax.fori_loop(start, stop, step, 0)


def back_columns(stacked, load_w):
    total = None
    for a in range(3):
        rows = jnp.concatenate(
            [stacked[2 - a : 6 - a, 2 - b : 18 - b].reshape(1024, 384) for b in range(3)], axis=1
        )
        filters = jnp.concatenate([load_w(9 * a + k) for k in range(9)], axis=1)
        term = lax.dot_general(rows, filters, (((1,), (1,)), ((), ())), preferred_element_type=F32)
        total = term if total is None else total + term
    return total


def backward_kernel(
    stacked_in, flipped2, slope, u1_in, u2, w1_in, w2_in,
    grad_in, grad1, grad2,
    u1, f1, f2, adj2, adj1, flipped1, rim2, rim1,
    terms2, far2a, near2a, mid2, far2b, near2b, total2,
    terms1, far1a, near1a, mid1, far1b, near1b, total1,
    hid_own, hid_bf, hid_sib, hid_sum, hid_got,
    inp_own, inp_bf, inp_sib, inp_sum, inp_got,
    g2s1, g2r1, g2s2, g2r2, g1s1, g1r1, g1s2, g1r2,
    h2s, h2r, h1s, h1r, hss, hsr, hys, hyr, iss, isr, iys, iyr, loc,
):
    s, c, x, z, y, core = place()
    loads = [
        pltpu.make_async_copy(stacked_in, adj2.at[1:5, 1:17], loc.at[0]),
        pltpu.make_async_copy(w2_in, f2, loc.at[1]),
        pltpu.make_async_copy(u1_in, u1, loc.at[2]),
        pltpu.make_async_copy(w1_in, f1, loc.at[3]),
    ]
    for copy in loads:
        copy.start()
    for field in (adj2, adj1):
        for row in (0, 17):
            field[:, row] = jnp.zeros((6, 16, 384), BF)
    for rim in (rim2, rim1):
        rim[...] = jnp.zeros_like(rim)
    greet(s, c, x, z)
    sibling = (s, y * 2 + 1 - core)

    middle = slice(128, 256)
    halo2 = Halo(
        s, c, stacked_in.at[0, :, :, middle], stacked_in.at[3, :, :, middle], rim2.at[0], rim2.at[1], h2s, h2r
    )

    def take_rims(halo, rim, field):
        halo.wait_recv()
        for side, plane in ((0, 0), (1, 5)):
            stack_shifts(rim[side].reshape(256, 128).astype(F32), plane, field, 0, 1)

    halo2.start()
    scatter2 = Scatter(
        terms2, far2a, near2a, mid2, far2b, near2b, total2, grad2, x, z, c, (g2s1, g2r1, g2s2, g2r2), 0
    )
    scatter1 = Scatter(
        terms1, far1a, near1a, mid1, far1b, near1b, total1, grad1, x, z, c, (g1s1, g1r1, g1s2, g1r2), 1
    )

    def second_chunk(j):
        a, b = lax.div(j, 3), lax.rem(j, 3)

        fields = [u2[q, pl.ds(a, 4), pl.ds(b, 16)].reshape(1024, 128) for q in range(8)]
        turned = dot(flipped2[...], jnp.concatenate(fields, axis=1)).T.astype(BF)
        for k in range(3):
            terms2[3 * j + k] = turned[:, k * 128 : (k + 1) * 128].reshape(4, 4, 64, 128)
        scatter2.start1(j)

    every_chunk(second_chunk, 0, 6)
    for copy in loads:
        copy.wait()
    take_rims(halo2, rim2, adj2)
    scatter2.relay1(0)
    scatter2.relay1(1)

    def hidden_to_sibling(n):
        return send(hid_bf.at[n, 1 - core], hid_sib.at[n], hss.at[n], hsr.at[n], sibling)

    def hidden_to_y(d):
        n = lax.rem(y + d, 4)
        return send(hid_sum.at[n], hid_got.at[d - 1], hys.at[d - 1], hyr.at[d - 1], (s, n * 2 + core))

    def hidden_pair(n):
        hidden_to_sibling(n).wait_recv()
        return hid_own[n] + hid_sib[n].astype(F32)

    def hidden_columns(i, _):
        n = lax.rem(y + 1 + i, 4)
        pl.when(i < 3)(lambda: second_chunk(jnp.minimum(6 + i, 8)))
        value = back_columns(adj2, lambda k: f2[k, n].reshape(256, 128))
        low, high = value[:, :128], value[:, 128:]
        hid_bf[n, 0] = low.astype(BF)
        hid_bf[n, 1] = high.astype(BF)
        hid_own[n] = jnp.where(core == 0, low, high)
        hidden_to_sibling(n).start()

        @pl.when(i > 0)
        def _():
            d = jnp.maximum(i, 1)
            before = lax.rem(y + d, 4)
            hid_sum[before] = hidden_pair(before).astype(BF)
            hidden_to_y(d).start()

        @pl.when(i < 3)
        def _():
            scatter2.relay1(2 * jnp.minimum(i, 2) + 2)
            scatter2.relay1(2 * jnp.minimum(i, 2) + 3)

        pl.when(i > 0)(lambda: scatter2.start2(jnp.maximum(i - 1, 0)))
        return 0

    lax.fori_loop(0, 4, hidden_columns, 0)
    hid_own[y] = hidden_pair(y)

    scatter2.start2(3)
    scatter2.start2(4)
    scatter2.relay1(8)
    for d in RING:
        hidden_to_y(d).wait_recv()
    for p in range(4):
        rows = slice(p * 256, (p + 1) * 256)
        value = hid_own[y, rows]
        for d in range(3):
            value = value + hid_got[d, rows].astype(F32)
        stack_shifts(value * slope[p], p, adj1, 1, 1, flipped1)
    halo1 = Halo(
        s, c, adj1.at[1, 1:17, :, middle], adj1.at[4, 1:17, :, middle], rim1.at[0], rim1.at[1], h1s, h1r
    )
    halo1.start()
    scatter2.relay2(0)
    scatter2.relay2(1)

    def first_chunk(j):
        a, b = lax.div(j, 3), lax.rem(j, 3)
        field = u1[pl.ds(a, 4), pl.ds(b, 16)].reshape(1024, 512)
        turned = dot(flipped1[...], field).T.astype(BF)
        for k in range(3):
            terms1[3 * j + k] = turned[:, k * 128 : (k + 1) * 128].reshape(4, 4, 32, 128)
        scatter1.start1(j)

    def first_step(j):
        first_chunk(j)
        pl.when(j > 4)(lambda: scatter1.relay1(jnp.maximum(j - 5, 0)))

    every_chunk(first_step)
    scatter2.start2(5)
    take_rims(halo1, rim1, adj1)
    scatter1.relay1(4)
    for n in range(2):
        value = back_columns(adj1, lambda k: f1[k, 2 * n : 2 * n + 2].reshape(256, 128))
        value = value.reshape(4, 4, 2, 2, 16, 256)
        columns = slice(n * 256, (n + 1) * 256)
        inp_own[:, :, :, :, :, columns] = value
        inp_bf[:, :, :, :, :, columns] = value.astype(BF)
        if n == 0:
            scatter1.start2(0)
            for j in (5, 6, 7):
                scatter1.relay1(j)
            scatter2.start2(6)
    to_sibling = send(inp_bf.at[:, :, 1 - core], inp_sib, iss.at[0], isr.at[0], sibling)
    to_sibling.start()

    def input_to_y(d):
        n = lax.rem(y + d, 4)
        return send(inp_sum.at[n], inp_got.at[d - 1], iys.at[d - 1], iyr.at[d - 1], (s, n * 2 + core))

    scatter1.relay1(8)
    scatter2.relay2(2)
    scatter2.relay2(3)
    scatter1.start2(1)
    scatter1.start2(2)
    scatter2.start2(7)
    to_sibling.wait_recv()
    for d in (1, 3, 2, 0):
        n = lax.rem(y + d, 4)
        pair = inp_own[:, n, core] + inp_sib[:, n].astype(F32)
        if d:
            inp_sum[n] = pair.astype(BF)
            input_to_y(d).start()
        else:
            grad_in[...] = pair
    for j in (3, 4, 5):
        scatter1.start2(j)
    scatter1.relay2(0)
    scatter2.relay2(4)
    scatter1.relay2(1)
    scatter2.start2(8)
    scatter1.start2(6)
    scatter1.relay2(2)
    scatter2.relay2(5)
    scatter1.start2(7)
    scatter1.relay2(3)
    scatter2.relay2(6)
    scatter1.start2(8)
    scatter1.relay2(4)
    scatter1.relay2(5)
    scatter2.relay2(7)
    scatter1.relay2(6)
    scatter2.relay2(8)
    scatter1.relay2(7)
    scatter1.relay2(8)
    every_chunk(scatter2.finish, 0, 7)
    for d in RING:
        input_to_y(d).wait_recv()
    value = grad_in[...]
    for d in range(3):
        value = value + inp_got[d].astype(F32)
    grad_in[...] = value
    every_chunk(scatter1.finish, 0, 6)
    every_chunk(scatter2.finish, 7, 9)
    every_chunk(scatter1.finish, 6, 9)

    halo2.wait_send()
    halo1.wait_send()
    to_sibling.wait_send()
    for n in range(4):
        hidden_to_sibling(n).wait_send()
    for d in RING:
        hidden_to_y(d).wait_send()
        input_to_y(d).wait_send()


def hand_over(*refs):
    for i in range(4):
        refs[4 + i][...] = refs[i][...]


def vmem(count):
    return [pl.BlockSpec(memory_space=pltpu.VMEM)] * count


def anywhere(count):
    return [pl.BlockSpec(memory_space=pl.ANY)] * count


def dma(*shape):
    return pltpu.SemaphoreType.DMA(shape)


def local(volume, w_first, b_first, w_second, b_second, cotangent):
    shape = jax.ShapeDtypeStruct
    flops = 2 * 1024 * 27 * 128 * 1536
    features, stacked, flipped, slope, u1, u2, f1, f2 = pl.pallas_call(
        forward_kernel,
        name="forward",
        out_shape=(
            shape((4, 16, 16, 128), BF),
            shape((4, 16, 16, 384), BF),
            shape((384, 1024), BF),
            shape((4, 256, 128), F32),
            shape((6, 18, 16, 512), BF),
            shape((8, 6, 18, 16, 128), BF),
            shape((27, 4, 4, 32, 128), BF),
            shape((27, 4, 4, 64, 128), BF),
        ),
        in_specs=vmem(1) + anywhere(1) + vmem(1) + anywhere(1) + vmem(2),
        out_specs=tuple(vmem(4) + anywhere(4)),
        scratch_shapes=[
            pltpu.VMEM((6, 18, 16, 512), BF),
            pltpu.VMEM((8, 6, 18, 16, 128), BF),
            pltpu.VMEM((27, 4, 4, 32, 128), BF),
            pltpu.VMEM((27, 4, 4, 64, 128), BF),
            pltpu.VMEM((1024, 384), F32),
            dma(2, 5, 4), dma(2, 5, 4), dma(3, 2, 5, 4), dma(3, 2, 5, 4),
            dma(2), dma(2), dma(2), dma(2),
            dma(4), dma(4), dma(4), dma(4), dma(3, 4), dma(3, 4), dma(3, 4), dma(3, 4),
            dma(8),
        ],
        compiler_params=pltpu.CompilerParams(
            collective_id=0, has_side_effects=True, vmem_limit_bytes=VMEM_BYTES
        ),
        cost_estimate=pl.CostEstimate(flops=flops, bytes_accessed=40_000_000, transcendentals=600_000),
    )(volume, w_first, b_first.reshape(1, 128), w_second, b_second.reshape(1, 128), cotangent)
    grad_input, grad_first, grad_second = pl.pallas_call(
        backward_kernel,
        name="backward",
        out_shape=(
            shape((4, 2, 16, 512), F32),
            shape((27, 32, 128), F32),
            shape((27, 64, 128), F32),
        ),
        in_specs=vmem(3) + anywhere(1) + vmem(1) + anywhere(2),
        out_specs=tuple(vmem(3)),
        scratch_shapes=[
            pltpu.VMEM((6, 18, 16, 512), BF),
            pltpu.VMEM((27, 4, 4, 32, 128), BF),
            pltpu.VMEM((27, 4, 4, 64, 128), BF),
            pltpu.VMEM((6, 18, 16, 384), BF),
            pltpu.VMEM((6, 18, 16, 384), BF),
            pltpu.VMEM((384, 1024), BF),
            pltpu.VMEM((2, 16, 16, 128), BF),
            pltpu.VMEM((2, 16, 16, 128), BF),
            pltpu.VMEM((27, 4, 4, 64, 128), BF),
            pltpu.VMEM((9, 2, 3, 2, 64, 128), BF),
            pltpu.VMEM((9, 2, 3, 4, 64, 128), BF),
            pltpu.VMEM((9, 3, 4, 64, 128), BF),
            pltpu.VMEM((9, 2, 3, 32, 128), BF),
            pltpu.VMEM((9, 2, 3, 64, 128), BF),
            pltpu.VMEM((3, 4, 64, 128), F32),
            pltpu.VMEM((27, 4, 4, 32, 128), BF),
            pltpu.VMEM((9, 2, 3, 2, 32, 128), BF),
            pltpu.VMEM((9, 2, 3, 4, 32, 128), BF),
            pltpu.VMEM((9, 3, 4, 32, 128), BF),
            pltpu.VMEM((9, 2, 3, 16, 128), BF),
            pltpu.VMEM((9, 2, 3, 32, 128), BF),
            pltpu.VMEM((3, 4, 32, 128), F32),
            pltpu.VMEM((4, 1024, 128), F32),
            pltpu.VMEM((4, 2, 1024, 128), BF),
            pltpu.VMEM((4, 1024, 128), BF),
            pltpu.VMEM((4, 1024, 128), BF),
            pltpu.VMEM((3, 1024, 128), BF),
            pltpu.VMEM((4, 4, 2, 2, 16, 512), F32),
            pltpu.VMEM((4, 4, 2, 2, 16, 512), BF),
            pltpu.VMEM((4, 4, 2, 16, 512), BF),
            pltpu.VMEM((4, 4, 2, 16, 512), BF),
            pltpu.VMEM((3, 4, 2, 16, 512), BF),
            dma(9, 4), dma(9, 4), dma(9, 4), dma(9, 4),
            dma(9, 4), dma(9, 4), dma(9, 4), dma(9, 4),
            dma(2), dma(2), dma(2), dma(2),
            dma(4), dma(4), dma(3), dma(3),
            dma(1), dma(1), dma(3), dma(3),
            dma(4),
        ],
        compiler_params=pltpu.CompilerParams(
            collective_id=1, has_side_effects=True, vmem_limit_bytes=VMEM_BYTES
        ),
        cost_estimate=pl.CostEstimate(flops=2 * flops, bytes_accessed=40_000_000, transcendentals=0),
    )(stacked, flipped, slope, u1, u2, f1, f2)
    results = (features, grad_input, grad_first, grad_second)
    return pl.pallas_call(
        hand_over,
        name="hand_over",
        out_shape=tuple(shape(r.shape, r.dtype) for r in results),
        in_specs=vmem(4),
        out_specs=tuple(vmem(4)),
        compiler_params=pltpu.CompilerParams(vmem_limit_bytes=VMEM_BYTES),
    )(*results)


def solution(mesh):
    return jax.shard_map(
        local,
        mesh=mesh,
        in_specs=(
            P("space", "chan", None, None),
            P(None, "space", "chan"),
            P("chan"),
            P(None, "space", "chan"),
            P("chan"),
            P("space", None, None, "chan"),
        ),
        out_specs=(
            P("space", None, None, "chan"),
            P("space", "chan", None, None),
            P(None, "space", "chan"),
            P(None, "space", "chan"),
        ),
        check_vma=False,
    )
```

```python
import functools

import jax
import jax.numpy as jnp
from jax import lax
from jax.experimental import pallas as pl
from jax.experimental.pallas import tpu as pltpu
from jax.sharding import PartitionSpec as P

MESH = pl.DeviceIdType.MESH
BF = jnp.bfloat16
F32 = jnp.float32
VMEM_BYTES = 63 * 1024 * 1024
RING = (1, 3, 2)
HALVES = ((0, 14), (14, 13))
THIRDS = (((0, 5), (5, 4)), ((9, 4), (13, 5)), ((18, 5), (23, 4)))


def place():
    s = lax.axis_index("space")
    c = lax.axis_index("chan")
    return s, c, lax.div(s, 4), lax.rem(s, 4), lax.div(c, 2), lax.rem(c, 2)


def send(src, dst, send_sem, recv_sem, target):
    return pltpu.make_async_remote_copy(
        src_ref=src,
        dst_ref=dst,
        send_sem=send_sem,
        recv_sem=recv_sem,
        device_id=target,
        device_id_type=MESH,
    )


def greet(s, c, x, z):
    barrier = pltpu.get_barrier_semaphore()

    def signal(space, chan):
        pl.semaphore_signal(barrier, inc=1, device_id=(space, chan), device_id_type=MESH)

    for d in (1, 2, 3):
        signal(lax.rem(x + d, 4) * 4 + z, c)
        signal(x * 4 + lax.rem(z + d, 4), c)
    for d in range(1, 8):
        signal(s, lax.rem(c + d, 8))

    @pl.when(s > 0)
    def _():
        signal(s - 1, c)

    @pl.when(s < 15)
    def _():
        signal(s + 1, c)

    inner = jnp.where(s > 0, 1, 0) + jnp.where(s < 15, 1, 0)
    pl.semaphore_wait(barrier, 13 + inner)


class Halo:
    def __init__(self, s, c, low_src, high_src, low_dst, high_dst, send_sem, recv_sem):
        self.s = s
        self.down = send(low_src, high_dst, send_sem.at[0], recv_sem.at[0], (jnp.maximum(s - 1, 0), c))
        self.up = send(high_src, low_dst, send_sem.at[1], recv_sem.at[1], (jnp.minimum(s + 1, 15), c))

    def start_down(self):
        pl.when(self.s > 0)(self.down.start)

    def start_up(self):
        pl.when(self.s < 15)(self.up.start)

    def start(self):
        self.start_down()
        self.start_up()

    def wait_recv(self):
        pl.when(self.s < 15)(self.down.wait_recv)
        pl.when(self.s > 0)(self.up.wait_recv)

    def wait_send(self):
        pl.when(self.s > 0)(self.down.wait_send)
        pl.when(self.s < 15)(self.up.wait_send)


HOPS = ((1, 0, 0), (3, 0, 0), (1, 1, 1), (3, 3, 2))


class Gather:
    def __init__(self, own, full, x, z, c, send_sem, recv_sem, halves):
        self.own, self.full, self.x, self.z, self.c, self.halves = own, full, x, z, c, halves
        self.send_sem, self.recv_sem = send_sem, recv_sem

    def span(self, half, part):
        k0, nk = self.halves[half]
        cut = (nk + 1) // 2
        return ((k0, nk), (k0, cut), (k0 + cut, nk - cut))[part]

    def region(self, half, first, second, part):
        ox = lax.rem(self.x + 4 - (second if half else first), 4)
        oz = lax.rem(self.z + 4 - (first if half else second), 4)
        k0, nk = self.span(half, part)
        return self.full.at[pl.ds(k0, nk), ox, oz]

    def copy(self, half, row, hop):
        step, behind_by, part = HOPS[hop]
        first, second = (behind_by, 0) if row == 0 else (row - 1, behind_by)
        dst = self.region(half, first, second, part)
        k0, nk = self.span(half, part)
        src = self.own.at[pl.ds(k0, nk)] if first == 0 and second == 0 else dst
        along_x = (row == 0) == (half == 0)
        tx = lax.rem(self.x + step, 4) if along_x else self.x
        tz = self.z if along_x else lax.rem(self.z + step, 4)
        return send(
            src, dst, self.send_sem.at[half, row, hop], self.recv_sem.at[half, row, hop], (tx * 4 + tz, self.c)
        )

    def arrived(self, half, row, hop):
        step, behind_by, part = HOPS[hop]
        distance = (step + behind_by) % 4
        first, second = (distance, 0) if row == 0 else (row - 1, distance)
        region = self.region(half, first, second, part)
        send(
            region,
            region,
            self.send_sem.at[half, row, hop],
            self.recv_sem.at[half, row, hop],
            (lax.rem(self.x + 1, 4) * 4 + self.z, self.c),
        ).wait_recv()

    def start_row(self, half, row):
        self.copy(half, row, 0).start()
        self.copy(half, row, 1).start()

    def start_own(self):
        for row in (0, 1):
            for half in (0, 1):
                self.start_row(half, row)

    def near(self):
        for hop, d in ((0, 1), (1, 3)):
            for half in (0, 1):
                self.arrived(half, 0, hop)
                self.copy(half, 0, hop + 2).start()
                self.start_row(half, 1 + d)

    def relay(self, d):
        for hop in (0, 1):
            for half in (0, 1):
                self.arrived(half, 1 + d, hop)
                self.copy(half, 1 + d, hop + 2).start()

    def far(self):
        for half in (0, 1):
            self.arrived(half, 0, 2)
            self.arrived(half, 0, 3)
            self.start_row(half, 3)

    def finish(self):
        for d in (0, 1, 3, 2):
            for half in (0, 1):
                self.arrived(half, 1 + d, 2)
                self.arrived(half, 1 + d, 3)

    def wait_send(self):
        for half in (0, 1):
            for row in range(5):
                for hop in range(4):
                    self.copy(half, row, hop).wait_send()


class ChanGather:
    def __init__(self, region, s, y, core, y_send, y_recv, c_send, c_recv):
        self.region, self.s, self.y, self.core = region, s, y, core
        self.sems = (y_send, y_recv, c_send, c_recv)

    def to_y(self, d):
        block = self.region(self.y * 2 + self.core)
        y_send, y_recv, _, _ = self.sems
        return send(
            block, block, y_send.at[d], y_recv.at[d], (self.s, lax.rem(self.y + d, 4) * 2 + self.core)
        )

    def from_y(self, d):
        block = self.region(lax.rem(self.y + 4 - d, 4) * 2 + self.core)
        y_send, y_recv, _, _ = self.sems
        return send(
            block, block, y_send.at[d], y_recv.at[d], (self.s, lax.rem(self.y + d, 4) * 2 + self.core)
        )

    def sibling(self, d, other):
        core = (1 - self.core) if other else self.core
        block = self.region(lax.rem(self.y + 4 - d, 4) * 2 + core)
        _, _, c_send, c_recv = self.sems
        return send(block, block, c_send.at[d], c_recv.at[d], (self.s, self.y * 2 + 1 - self.core))

    def start_own(self):
        for d in RING:
            self.to_y(d).start()
        self.sibling(0, False).start()

    def forward(self):
        for d in RING:
            self.from_y(d).wait_recv()
            self.sibling(d, False).start()

    def finish(self):
        for d in range(4):
            self.sibling(d, True).wait_recv()

    def wait_send(self):
        for d in RING:
            self.to_y(d).wait_send()
        for d in range(4):
            self.sibling(d, False).wait_send()


def z_mask(last):
    row = lax.broadcasted_iota(jnp.int32, (256, 128), 0)
    return lax.rem(row, 16) != (15 if last else 0)


def behind(v):
    return jnp.where(z_mask(False), pltpu.roll(v, 1, 0), 0.0)


def ahead(v):
    return jnp.where(z_mask(True), pltpu.roll(v, 255, 0), 0.0)


def slope_of(v):
    sigma = jax.nn.sigmoid(v)
    return sigma * (1.0 + v * (1.0 - sigma))


def stack_shifts(v, xp, stacked, x0, y0, flipped=None):
    for k, shifted in enumerate((ahead(v), v, behind(v))):
        stacked[xp + x0, y0 : y0 + 16, :, k * 128 : (k + 1) * 128] = shifted.astype(BF).reshape(16, 16, 128)
        if flipped is not None:
            flipped[k * 128 : (k + 1) * 128, xp * 256 : (xp + 1) * 256] = shifted.T.astype(BF)


def dot(a, b):
    return jnp.dot(a, b, preferred_element_type=F32)


def convolve_part(load, load_w, a, acc):
    rows = jnp.concatenate([load(a, b) for b in range(3)], axis=1)
    filters = jnp.concatenate(
        [jnp.concatenate([load_w(9 * a + 3 * b + k) for k in range(3)], axis=1) for b in range(3)], axis=0
    )
    acc[...] += dot(rows, filters)


def plane_of(acc, index):
    rows = slice(index * 256, (index + 1) * 256)
    return behind(acc[rows, 0:128]) + acc[rows, 128:256] + ahead(acc[rows, 256:384])


class Scatter:
    def __init__(self, terms, far1, near1, mid, far2, near2, total, out, x, z, c, sems, flip):
        self.terms, self.far1, self.near1 = terms, far1, near1
        self.mid, self.far2, self.near2 = mid, far2, near2
        self.total, self.out = total, out
        self.x, self.z, self.c, self.flip = x, z, c, flip
        self.s1, self.r1, self.s2, self.r2 = sems
        self.rows = out.shape[1]

    def by_axis(self, j, act):
        if isinstance(j, int):
            return act((j + self.flip) % 2 == 0)
        x_first = lax.rem(j + self.flip, 2) == 0

        @pl.when(x_first)
        def _():
            act(True)

        @pl.when(jnp.logical_not(x_first))
        def _():
            act(False)

    def target(self, along_x, d):
        tx = lax.rem(self.x + d, 4) if along_x else self.x
        tz = self.z if along_x else lax.rem(self.z + d, 4)
        return tx * 4 + tz, self.c

    def block1(self, j, x_first, d, part=None):
        offsets = pl.ds(3 * j, 3)
        if x_first:
            lead = (offsets, lax.rem(self.x + d, 4))
            return lead if part is None else lead + (slice(2 * part, 2 * part + 2),)
        at = lax.rem(self.z + d, 4)
        return (offsets, slice(None) if part is None else slice(2 * part, 2 * part + 2), at)

    def block2(self, j, x_first, d, part=None):
        at = lax.rem((self.z if x_first else self.x) + d, 4)
        half = self.rows // 2
        lead = (j, slice(None), at)
        return lead if part is None else lead + (slice(half * part, half * (part + 1)),)

    def far(self, stage, j, x_first, way):
        src, dst = (
            (self.terms.at[self.block1(j, x_first, 2, way)], self.far1)
            if stage == 1
            else (self.mid.at[self.block2(j, x_first, 2, way)], self.far2)
        )
        s, r = (self.s1, self.r1) if stage == 1 else (self.s2, self.r2)
        to = self.target(x_first == (stage == 1), (1, 3)[way])
        return send(src, dst.at[j, way], s.at[j, way], r.at[j, way], to)

    def near(self, stage, j, x_first, way):
        step = (1, 3)[way]
        src, dst = (
            (self.terms.at[self.block1(j, x_first, step)], self.near1)
            if stage == 1
            else (self.mid.at[self.block2(j, x_first, step)], self.near2)
        )
        s, r = (self.s1, self.r1) if stage == 1 else (self.s2, self.r2)
        to = self.target(x_first == (stage == 1), step)
        return send(src, dst.at[j, way], s.at[j, 2 + way], r.at[j, 2 + way], to)

    def pass_on(self, stage, j, x_first):
        for way, step in ((0, 1), (1, 3)):
            self.far(stage, j, x_first, way).wait_recv()
            if stage == 1:
                field, got, where = self.terms, self.far1, self.block1(j, x_first, step, way)
            else:
                field, got, where = self.mid, self.far2, self.block2(j, x_first, step, way)
            field[where] = (field[where].astype(F32) + got[j, way].astype(F32)).astype(BF)
            self.near(stage, j, x_first, way).start()

    def start1(self, j):
        def act(x_first):
            self.far(1, j, x_first, 0).start()
            self.far(1, j, x_first, 1).start()

        self.by_axis(j, act)

    def relay1(self, j):
        self.by_axis(j, lambda x_first: self.pass_on(1, j, x_first))

    def start2(self, j):
        def act(x_first):
            value = self.terms[self.block1(j, x_first, 0)].astype(F32)
            for way in (0, 1):
                self.near(1, j, x_first, way).wait_recv()
                value = value + self.near1[j, way].astype(F32)
            self.total[...] = value
            self.mid[j] = value.astype(BF)
            self.far(2, j, x_first, 0).start()
            self.far(2, j, x_first, 1).start()
            self.out[pl.ds(3 * j, 3)] = self.total[:, self.z] if x_first else self.total[:, self.x]

        self.by_axis(j, act)

    def relay2(self, j):
        self.by_axis(j, lambda x_first: self.pass_on(2, j, x_first))

    def finish(self, j):
        def act(x_first):
            value = self.out[pl.ds(3 * j, 3)]
            for way in (0, 1):
                self.near(2, j, x_first, way).wait_recv()
                value = value + self.near2[j, way].astype(F32)
            self.out[pl.ds(3 * j, 3)] = value
            for stage in (1, 2):
                for way in (0, 1):
                    self.far(stage, j, x_first, way).wait_send()
                    self.near(stage, j, x_first, way).wait_send()

        self.by_axis(j, act)


def every_chunk(act, start=0, stop=9):
    def step(j, _):
        act(j)
        return 0

    lax.fori_loop(start, stop, step, 0)


def back_columns(stacked, load_w):
    total = None
    for a in range(3):
        rows = jnp.concatenate(
            [stacked[2 - a : 6 - a, 2 - b : 18 - b].reshape(1024, 384) for b in range(3)], axis=1
        )
        filters = jnp.concatenate([load_w(9 * a + k) for k in range(9)], axis=1)
        term = lax.dot_general(rows, filters, (((1,), (1,)), ((), ())), preferred_element_type=F32)
        total = term if total is None else total + term
    return total


def step_kernel(
    vol, w1, b1, w2, b2, cot,
    feat, grad_in, grad1, grad2,
    u1, u2, f1, f2, acc, slope,
    adj2, adj1, flipped2, flipped1, rim2, rim1,
    terms2, far2a, near2a, mid2, far2b, near2b, total2,
    terms1, far1a, near1a, mid1, far1b, near1b, total1,
    hid_own, hid_bf, hid_sib, hid_sum, hid_got,
    inp_own, inp_bf, inp_sib, inp_sum, inp_got,
    ag1_s, ag1_r, ag2_s, ag2_r, halo_s, halo_r, hh_s, hh_r, y_s, y_r, c_s, c_r, hy_s, hy_r, hc_s, hc_r, loc,
    g2s1, g2r1, g2s2, g2r2, g1s1, g1r1, g1s2, g1r2,
    h2s, h2r, h1s, h1r, hss, hsr, hys, hyr, iss, isr, iys, iyr,
):
    s, c, x, z, y, core = place()
    u1[0] = jnp.zeros((18, 16, 512), BF)
    u1[5] = jnp.zeros((18, 16, 512), BF)
    for row in (0, 17):
        u1[1:5, row] = jnp.zeros((4, 16, 512), BF)

    def clear(b, _):
        u2[b, 0] = jnp.zeros((18, 16, 128), BF)
        u2[b, 5] = jnp.zeros((18, 16, 128), BF)
        for row in (0, 17):
            u2[b, 1:5, row] = jnp.zeros((4, 16, 128), BF)
        return 0

    lax.fori_loop(0, 8, clear, 0)
    for field in (adj2, adj1):
        for row in (0, 17):
            field[:, row] = jnp.zeros((6, 16, 384), BF)
    for rim in (rim2, rim1):
        rim[...] = jnp.zeros_like(rim)
    rows_of = lambda cb: u1.at[:, pl.ds(1 + 2 * cb, 2)]
    locals_ = [
        pltpu.make_async_copy(vol, u1.at[1:5, pl.ds(1 + 2 * c, 2)], loc.at[0]),
        pltpu.make_async_copy(w1, f1.at[:, x, z], loc.at[1]),
        pltpu.make_async_copy(w2, f2.at[:, x, z], loc.at[2]),
    ]
    for copy in locals_:
        copy.start()
    greet(s, c, x, z)

    first = Gather(w1, f1, x, z, c, ag1_s, ag1_r, HALVES)
    second = [Gather(w2, f2, x, z, c, ag2_s.at[i], ag2_r.at[i], THIRDS[i]) for i in range(3)]
    halo = Halo(
        s, c, vol.at[0], vol.at[3],
        u1.at[0, pl.ds(1 + 2 * c, 2)], u1.at[5, pl.ds(1 + 2 * c, 2)], halo_s, halo_r,
    )
    voxels = ChanGather(rows_of, s, y, core, y_s, y_r, c_s, c_r)
    halo.start()
    first.start_own()
    locals_[0].wait()
    halo.wait_recv()
    first.near()
    voxels.start_own()
    first.relay(0)
    first.far()
    first.relay(1)
    first.relay(3)
    voxels.forward()
    first.relay(2)
    voxels.finish()
    second[0].start_own()
    second[1].start_own()
    locals_[1].wait()
    locals_[2].wait()
    acc[...] = jnp.zeros_like(acc)
    first.finish()

    hidden_halo = Halo(
        s, c, u2.at[c, 1, 1:17], u2.at[c, 4, 1:17], u2.at[c, 0, 1:17], u2.at[c, 5, 1:17], hh_s, hh_r
    )
    for a in range(3):
        convolve_part(
            lambda a, b: u1[a : a + 4, b : b + 16].reshape(1024, 512),
            lambda k: f1[k].reshape(512, 128),
            a,
            acc,
        )
        if a == 0:
            second[0].near()
    for p in (0, 3, 1, 2):
        pre = plane_of(acc, p) + b1[...]
        slope[p] = slope_of(pre)
        u2[c, p + 1, 1:17] = (pre * jax.nn.sigmoid(pre)).astype(BF).reshape(16, 16, 128)
        if p == 3:
            hidden_halo.start()
            second[2].start_own()
    channels, low_rim, high_rim = [
        ChanGather(
            lambda cb, planes=planes: u2.at[cb, planes, 1:17],
            s, y, core, hy_s.at[i], hy_r.at[i], hc_s.at[i], hc_r.at[i],
        )
        for i, planes in enumerate((slice(1, 5), 0, 5))
    ]
    channels.start_own()
    second[0].relay(3)
    second[1].near()
    acc[...] = jnp.zeros_like(acc)
    second[2].near()
    hidden_halo.wait_recv()
    low_rim.start_own()
    high_rim.start_own()
    second[0].far()
    second[0].relay(0)
    second[1].far()
    channels.forward()
    second[0].relay(1)
    second[1].relay(0)
    second[0].relay(2)
    second[1].relay(3)
    low_rim.forward()
    high_rim.forward()
    second[1].relay(1)
    second[2].far()
    channels.finish()
    low_rim.finish()
    high_rim.finish()
    second[1].relay(2)
    second[2].relay(3)
    second[2].relay(1)
    second[0].finish()
    second[2].relay(0)
    for a in range(3):
        convolve_part(
            lambda a, b: jnp.concatenate(
                [u2[q, a : a + 4, b : b + 16].reshape(1024, 128) for q in range(8)], axis=1
            ),
            lambda k: f2[k].reshape(1024, 128),
            a,
            acc,
        )
        if a < 2:
            second[a + 1].finish()
        if a == 0:
            second[2].relay(2)
    middle = slice(128, 256)
    halo2 = Halo(
        s, c, adj2.at[1, 1:17, :, middle], adj2.at[4, 1:17, :, middle], rim2.at[0], rim2.at[1], h2s, h2r
    )
    for p in (0, 3, 1, 2):
        pre = plane_of(acc, p) + b2[...]
        feat[p] = (pre * jax.nn.sigmoid(pre)).astype(BF).reshape(16, 16, 128)
        adjoint = cot[p].reshape(256, 128).astype(F32) * slope_of(pre)
        stack_shifts(adjoint, p, adj2, 1, 1, flipped2)
        if p == 3:
            halo2.start()
    sibling = (s, y * 2 + 1 - core)

    def take_rims(halo, rim, field):
        halo.wait_recv()
        for side, plane in ((0, 0), (1, 5)):
            stack_shifts(rim[side].reshape(256, 128).astype(F32), plane, field, 0, 1)

    scatter2 = Scatter(
        terms2, far2a, near2a, mid2, far2b, near2b, total2, grad2, x, z, c, (g2s1, g2r1, g2s2, g2r2), 0
    )
    scatter1 = Scatter(
        terms1, far1a, near1a, mid1, far1b, near1b, total1, grad1, x, z, c, (g1s1, g1r1, g1s2, g1r2), 1
    )

    def second_chunk(j):
        a, b = lax.div(j, 3), lax.rem(j, 3)

        fields = [u2[q, pl.ds(a, 4), pl.ds(b, 16)].reshape(1024, 128) for q in range(8)]
        turned = dot(flipped2[...], jnp.concatenate(fields, axis=1)).T.astype(BF)
        for k in range(3):
            terms2[3 * j + k] = turned[:, k * 128 : (k + 1) * 128].reshape(4, 4, 64, 128)
        scatter2.start1(j)

    every_chunk(second_chunk, 0, 6)
    take_rims(halo2, rim2, adj2)
    scatter2.relay1(0)
    scatter2.relay1(1)

    def hidden_to_sibling(n):
        return send(hid_bf.at[n, 1 - core], hid_sib.at[n], hss.at[n], hsr.at[n], sibling)

    def hidden_to_y(d):
        n = lax.rem(y + d, 4)
        return send(hid_sum.at[n], hid_got.at[d - 1], hys.at[d - 1], hyr.at[d - 1], (s, n * 2 + core))

    def hidden_pair(n):
        hidden_to_sibling(n).wait_recv()
        return hid_own[n] + hid_sib[n].astype(F32)

    def hidden_columns(i, _):
        n = lax.rem(y + 1 + i, 4)
        pl.when(i < 3)(lambda: second_chunk(jnp.minimum(6 + i, 8)))
        value = back_columns(adj2, lambda k: f2[k, n].reshape(256, 128))
        low, high = value[:, :128], value[:, 128:]
        hid_bf[n, 0] = low.astype(BF)
        hid_bf[n, 1] = high.astype(BF)
        hid_own[n] = jnp.where(core == 0, low, high)
        hidden_to_sibling(n).start()

        @pl.when(i > 0)
        def _():
            d = jnp.maximum(i, 1)
            before = lax.rem(y + d, 4)
            hid_sum[before] = hidden_pair(before).astype(BF)
            hidden_to_y(d).start()

        @pl.when(i < 3)
        def _():
            scatter2.relay1(2 * jnp.minimum(i, 2) + 2)
            scatter2.relay1(2 * jnp.minimum(i, 2) + 3)

        pl.when(i > 0)(lambda: scatter2.start2(jnp.maximum(i - 1, 0)))
        return 0

    lax.fori_loop(0, 4, hidden_columns, 0)
    hid_own[y] = hidden_pair(y)

    scatter2.start2(3)
    scatter2.start2(4)
    scatter2.relay1(8)
    for d in RING:
        hidden_to_y(d).wait_recv()
    for p in range(4):
        rows = slice(p * 256, (p + 1) * 256)
        value = hid_own[y, rows]
        for d in range(3):
            value = value + hid_got[d, rows].astype(F32)
        stack_shifts(value * slope[p], p, adj1, 1, 1, flipped1)
    halo1 = Halo(
        s, c, adj1.at[1, 1:17, :, middle], adj1.at[4, 1:17, :, middle], rim1.at[0], rim1.at[1], h1s, h1r
    )
    halo1.start()
    scatter2.relay2(0)
    scatter2.relay2(1)

    def first_chunk(j):
        a, b = lax.div(j, 3), lax.rem(j, 3)
        field = u1[pl.ds(a, 4), pl.ds(b, 16)].reshape(1024, 512)
        turned = dot(flipped1[...], field).T.astype(BF)
        for k in range(3):
            terms1[3 * j + k] = turned[:, k * 128 : (k + 1) * 128].reshape(4, 4, 32, 128)
        scatter1.start1(j)

    def first_step(j):
        first_chunk(j)
        pl.when(j > 4)(lambda: scatter1.relay1(jnp.maximum(j - 5, 0)))

    every_chunk(first_step)
    scatter2.start2(5)
    take_rims(halo1, rim1, adj1)
    scatter1.relay1(4)
    for n in range(2):
        value = back_columns(adj1, lambda k: f1[k, 2 * n : 2 * n + 2].reshape(256, 128))
        value = value.reshape(4, 4, 2, 2, 16, 256)
        columns = slice(n * 256, (n + 1) * 256)
        inp_own[:, :, :, :, :, columns] = value
        inp_bf[:, :, :, :, :, columns] = value.astype(BF)
        if n == 0:
            scatter1.start2(0)
            for j in (5, 6, 7):
                scatter1.relay1(j)
            scatter2.start2(6)
    to_sibling = send(inp_bf.at[:, :, 1 - core], inp_sib, iss.at[0], isr.at[0], sibling)
    to_sibling.start()

    def input_to_y(d):
        n = lax.rem(y + d, 4)
        return send(inp_sum.at[n], inp_got.at[d - 1], iys.at[d - 1], iyr.at[d - 1], (s, n * 2 + core))

    scatter1.relay1(8)
    scatter2.relay2(2)
    scatter2.relay2(3)
    scatter1.start2(1)
    scatter1.start2(2)
    scatter2.start2(7)
    to_sibling.wait_recv()
    for d in (1, 3, 2, 0):
        n = lax.rem(y + d, 4)
        pair = inp_own[:, n, core] + inp_sib[:, n].astype(F32)
        if d:
            inp_sum[n] = pair.astype(BF)
            input_to_y(d).start()
        else:
            grad_in[...] = pair
    for j in (3, 4, 5):
        scatter1.start2(j)
    scatter1.relay2(0)
    scatter2.relay2(4)
    scatter1.relay2(1)
    scatter2.start2(8)
    scatter1.start2(6)
    scatter1.relay2(2)
    scatter2.relay2(5)
    scatter1.start2(7)
    scatter1.relay2(3)
    scatter2.relay2(6)
    scatter1.start2(8)
    scatter1.relay2(4)
    scatter1.relay2(5)
    scatter2.relay2(7)
    scatter1.relay2(6)
    scatter2.relay2(8)
    scatter1.relay2(7)
    scatter1.relay2(8)
    every_chunk(scatter2.finish, 0, 7)
    for d in RING:
        input_to_y(d).wait_recv()
    value = grad_in[...]
    for d in range(3):
        value = value + inp_got[d].astype(F32)
    grad_in[...] = value
    every_chunk(scatter1.finish, 0, 6)
    every_chunk(scatter2.finish, 7, 9)
    every_chunk(scatter1.finish, 6, 9)

    halo2.wait_send()
    halo1.wait_send()
    to_sibling.wait_send()
    for n in range(4):
        hidden_to_sibling(n).wait_send()
    for d in RING:
        hidden_to_y(d).wait_send()
        input_to_y(d).wait_send()
    halo.wait_send()
    hidden_halo.wait_send()
    voxels.wait_send()
    for part in (channels, low_rim, high_rim):
        part.wait_send()
    first.wait_send()
    for part in second:
        part.wait_send()


def hand_over(*refs):
    for i in range(4):
        refs[4 + i][...] = refs[i][...]


def vmem(count):
    return [pl.BlockSpec(memory_space=pltpu.VMEM)] * count


def anywhere(count):
    return [pl.BlockSpec(memory_space=pl.ANY)] * count


def dma(*shape):
    return pltpu.SemaphoreType.DMA(shape)


def local(volume, w_first, b_first, w_second, b_second, cotangent):
    shape = jax.ShapeDtypeStruct
    flops = 2 * 1024 * 27 * 128 * 1536
    half_banks = lambda rows: [
        pltpu.VMEM((27, 4, 4, rows, 128), BF),
        pltpu.VMEM((9, 2, 3, 2, rows, 128), BF),
        pltpu.VMEM((9, 2, 3, 4, rows, 128), BF),
        pltpu.VMEM((9, 3, 4, rows, 128), BF),
        pltpu.VMEM((9, 2, 3, rows // 2, 128), BF),
        pltpu.VMEM((9, 2, 3, rows, 128), BF),
        pltpu.VMEM((3, 4, rows, 128), F32),
    ]
    features, grad_input, grad_first, grad_second = pl.pallas_call(
        step_kernel,
        name="forward_backward",
        out_shape=(
            shape((4, 16, 16, 128), BF),
            shape((4, 2, 16, 512), F32),
            shape((27, 32, 128), F32),
            shape((27, 64, 128), F32),
        ),
        in_specs=vmem(1) + anywhere(1) + vmem(1) + anywhere(1) + vmem(2),
        out_specs=tuple(vmem(4)),
        scratch_shapes=[
            pltpu.VMEM((6, 18, 16, 512), BF),
            pltpu.VMEM((8, 6, 18, 16, 128), BF),
            pltpu.VMEM((27, 4, 4, 32, 128), BF),
            pltpu.VMEM((27, 4, 4, 64, 128), BF),
            pltpu.VMEM((1024, 384), F32),
            pltpu.VMEM((4, 256, 128), F32),
            pltpu.VMEM((6, 18, 16, 384), BF),
            pltpu.VMEM((6, 18, 16, 384), BF),
            pltpu.VMEM((384, 1024), BF),
            pltpu.VMEM((384, 1024), BF),
            pltpu.VMEM((2, 16, 16, 128), BF),
            pltpu.VMEM((2, 16, 16, 128), BF),
            *half_banks(64),
            *half_banks(32),
            pltpu.VMEM((4, 1024, 128), F32),
            pltpu.VMEM((4, 2, 1024, 128), BF),
            pltpu.VMEM((4, 1024, 128), BF),
            pltpu.VMEM((4, 1024, 128), BF),
            pltpu.VMEM((3, 1024, 128), BF),
            pltpu.VMEM((4, 4, 2, 2, 16, 512), F32),
            pltpu.VMEM((4, 4, 2, 2, 16, 512), BF),
            pltpu.VMEM((4, 4, 2, 16, 512), BF),
            pltpu.VMEM((4, 4, 2, 16, 512), BF),
            pltpu.VMEM((3, 4, 2, 16, 512), BF),
            dma(2, 5, 4), dma(2, 5, 4), dma(3, 2, 5, 4), dma(3, 2, 5, 4),
            dma(2), dma(2), dma(2), dma(2),
            dma(4), dma(4), dma(4), dma(4), dma(3, 4), dma(3, 4), dma(3, 4), dma(3, 4),
            dma(3),
            dma(9, 4), dma(9, 4), dma(9, 4), dma(9, 4),
            dma(9, 4), dma(9, 4), dma(9, 4), dma(9, 4),
            dma(2), dma(2), dma(2), dma(2),
            dma(4), dma(4), dma(3), dma(3),
            dma(1), dma(1), dma(3), dma(3),
        ],
        compiler_params=pltpu.CompilerParams(
            collective_id=0, has_side_effects=True, vmem_limit_bytes=VMEM_BYTES
        ),
        cost_estimate=pl.CostEstimate(flops=3 * flops, bytes_accessed=8_000_000, transcendentals=600_000),
    )(volume, w_first, b_first.reshape(1, 128), w_second, b_second.reshape(1, 128), cotangent)
    results = (features, grad_input, grad_first, grad_second)
    return pl.pallas_call(
        hand_over,
        name="hand_over",
        out_shape=tuple(shape(r.shape, r.dtype) for r in results),
        in_specs=vmem(4),
        out_specs=tuple(vmem(4)),
        compiler_params=pltpu.CompilerParams(vmem_limit_bytes=VMEM_BYTES),
    )(*results)


def solution(mesh):
    return jax.shard_map(
        local,
        mesh=mesh,
        in_specs=(
            P("space", "chan", None, None),
            P(None, "space", "chan"),
            P("chan"),
            P(None, "space", "chan"),
            P("chan"),
            P("space", None, None, "chan"),
        ),
        out_specs=(
            P("space", None, None, "chan"),
            P("space", "chan", None, None),
            P(None, "space", "chan"),
            P(None, "space", "chan"),
        ),
        check_vma=False,
    )
```

```python
import functools

import jax
import jax.numpy as jnp
from jax import lax
from jax.experimental import pallas as pl
from jax.experimental.pallas import tpu as pltpu
from jax.sharding import PartitionSpec as P

MESH = pl.DeviceIdType.MESH
BF = jnp.bfloat16
F32 = jnp.float32
VMEM_BYTES = 63 * 1024 * 1024
RING = (1, 3, 2)
HALVES = ((0, 14), (14, 13))
THIRDS = (((0, 5), (5, 4)), ((9, 4), (13, 5)), ((18, 5), (23, 4)))


def place():
    s = lax.axis_index("space")
    c = lax.axis_index("chan")
    return s, c, lax.div(s, 4), lax.rem(s, 4), lax.div(c, 2), lax.rem(c, 2)


def send(src, dst, send_sem, recv_sem, target):
    return pltpu.make_async_remote_copy(
        src_ref=src,
        dst_ref=dst,
        send_sem=send_sem,
        recv_sem=recv_sem,
        device_id=target,
        device_id_type=MESH,
    )


def greet(s, c, x, z):
    barrier = pltpu.get_barrier_semaphore()

    def signal(space, chan):
        pl.semaphore_signal(barrier, inc=1, device_id=(space, chan), device_id_type=MESH)

    for d in (1, 2, 3):
        signal(lax.rem(x + d, 4) * 4 + z, c)
        signal(x * 4 + lax.rem(z + d, 4), c)
    for d in range(1, 8):
        signal(s, lax.rem(c + d, 8))

    @pl.when(s > 0)
    def _():
        signal(s - 1, c)

    @pl.when(s < 15)
    def _():
        signal(s + 1, c)

    inner = jnp.where(s > 0, 1, 0) + jnp.where(s < 15, 1, 0)
    pl.semaphore_wait(barrier, 13 + inner)


class Halo:
    def __init__(self, s, c, low_src, high_src, low_dst, high_dst, send_sem, recv_sem):
        self.s = s
        self.down = send(low_src, high_dst, send_sem.at[0], recv_sem.at[0], (jnp.maximum(s - 1, 0), c))
        self.up = send(high_src, low_dst, send_sem.at[1], recv_sem.at[1], (jnp.minimum(s + 1, 15), c))

    def start_down(self):
        pl.when(self.s > 0)(self.down.start)

    def start_up(self):
        pl.when(self.s < 15)(self.up.start)

    def start(self):
        self.start_down()
        self.start_up()

    def wait_recv(self):
        pl.when(self.s < 15)(self.down.wait_recv)
        pl.when(self.s > 0)(self.up.wait_recv)

    def wait_send(self):
        pl.when(self.s > 0)(self.down.wait_send)
        pl.when(self.s < 15)(self.up.wait_send)


HOPS = ((1, 0, 0), (3, 0, 0), (1, 1, 1), (3, 3, 2))


class Gather:
    def __init__(self, own, full, x, z, c, send_sem, recv_sem, halves):
        self.own, self.full, self.x, self.z, self.c, self.halves = own, full, x, z, c, halves
        self.send_sem, self.recv_sem = send_sem, recv_sem

    def span(self, half, part):
        k0, nk = self.halves[half]
        cut = (nk + 1) // 2
        return ((k0, nk), (k0, cut), (k0 + cut, nk - cut))[part]

    def region(self, half, first, second, part):
        ox = lax.rem(self.x + 4 - (second if half else first), 4)
        oz = lax.rem(self.z + 4 - (first if half else second), 4)
        k0, nk = self.span(half, part)
        return self.full.at[pl.ds(k0, nk), ox, oz]

    def copy(self, half, row, hop):
        step, behind_by, part = HOPS[hop]
        first, second = (behind_by, 0) if row == 0 else (row - 1, behind_by)
        dst = self.region(half, first, second, part)
        k0, nk = self.span(half, part)
        src = self.own.at[pl.ds(k0, nk)] if first == 0 and second == 0 else dst
        along_x = (row == 0) == (half == 0)
        tx = lax.rem(self.x + step, 4) if along_x else self.x
        tz = self.z if along_x else lax.rem(self.z + step, 4)
        return send(
            src, dst, self.send_sem.at[half, row, hop], self.recv_sem.at[half, row, hop], (tx * 4 + tz, self.c)
        )

    def arrived(self, half, row, hop):
        step, behind_by, part = HOPS[hop]
        distance = (step + behind_by) % 4
        first, second = (distance, 0) if row == 0 else (row - 1, distance)
        region = self.region(half, first, second, part)
        send(
            region,
            region,
            self.send_sem.at[half, row, hop],
            self.recv_sem.at[half, row, hop],
            (lax.rem(self.x + 1, 4) * 4 + self.z, self.c),
        ).wait_recv()

    def start_row(self, half, row):
        self.copy(half, row, 0).start()
        self.copy(half, row, 1).start()

    def start_own(self):
        for row in (0, 1):
            for half in (0, 1):
                self.start_row(half, row)

    def near(self):
        for hop, d in ((0, 1), (1, 3)):
            for half in (0, 1):
                self.arrived(half, 0, hop)
                self.copy(half, 0, hop + 2).start()
                self.start_row(half, 1 + d)

    def relay(self, d):
        for hop in (0, 1):
            for half in (0, 1):
                self.arrived(half, 1 + d, hop)
                self.copy(half, 1 + d, hop + 2).start()

    def far(self):
        for half in (0, 1):
            self.arrived(half, 0, 2)
            self.arrived(half, 0, 3)
            self.start_row(half, 3)

    def finish(self):
        for d in (0, 1, 3, 2):
            for half in (0, 1):
                self.arrived(half, 1 + d, 2)
                self.arrived(half, 1 + d, 3)

    def wait_send(self):
        for half in (0, 1):
            for row in range(5):
                for hop in range(4):
                    self.copy(half, row, hop).wait_send()


class ChanGather:
    def __init__(self, region, s, y, core, y_send, y_recv, c_send, c_recv):
        self.region, self.s, self.y, self.core = region, s, y, core
        self.sems = (y_send, y_recv, c_send, c_recv)

    def to_y(self, d):
        block = self.region(self.y * 2 + self.core)
        y_send, y_recv, _, _ = self.sems
        return send(
            block, block, y_send.at[d], y_recv.at[d], (self.s, lax.rem(self.y + d, 4) * 2 + self.core)
        )

    def from_y(self, d):
        block = self.region(lax.rem(self.y + 4 - d, 4) * 2 + self.core)
        y_send, y_recv, _, _ = self.sems
        return send(
            block, block, y_send.at[d], y_recv.at[d], (self.s, lax.rem(self.y + d, 4) * 2 + self.core)
        )

    def sibling(self, d, other):
        core = (1 - self.core) if other else self.core
        block = self.region(lax.rem(self.y + 4 - d, 4) * 2 + core)
        _, _, c_send, c_recv = self.sems
        return send(block, block, c_send.at[d], c_recv.at[d], (self.s, self.y * 2 + 1 - self.core))

    def start_own(self):
        for d in RING:
            self.to_y(d).start()
        self.sibling(0, False).start()

    def forward(self):
        for d in RING:
            self.from_y(d).wait_recv()
            self.sibling(d, False).start()

    def finish(self):
        for d in range(4):
            self.sibling(d, True).wait_recv()

    def wait_send(self):
        for d in RING:
            self.to_y(d).wait_send()
        for d in range(4):
            self.sibling(d, False).wait_send()


def z_mask(last):
    row = lax.broadcasted_iota(jnp.int32, (256, 128), 0)
    return lax.rem(row, 16) != (15 if last else 0)


def behind(v):
    return jnp.where(z_mask(False), pltpu.roll(v, 1, 0), 0.0)


def ahead(v):
    return jnp.where(z_mask(True), pltpu.roll(v, 255, 0), 0.0)


def slope_of(v):
    sigma = jax.nn.sigmoid(v)
    return sigma * (1.0 + v * (1.0 - sigma))


def stack_shifts(v, xp, stacked, x0, y0, flipped=None):
    for k, shifted in enumerate((ahead(v), v, behind(v))):
        stacked[xp + x0, y0 : y0 + 16, :, k * 128 : (k + 1) * 128] = shifted.astype(BF).reshape(16, 16, 128)
        if flipped is not None:
            flipped[k * 128 : (k + 1) * 128, xp * 256 : (xp + 1) * 256] = shifted.T.astype(BF)


def dot(a, b):
    return jnp.dot(a, b, preferred_element_type=F32)


def convolve_part(load, load_w, a, acc):
    rows = jnp.concatenate([load(a, b) for b in range(3)], axis=1)
    filters = jnp.concatenate(
        [jnp.concatenate([load_w(9 * a + 3 * b + k) for k in range(3)], axis=1) for b in range(3)], axis=0
    )
    acc[...] += dot(rows, filters)


def plane_of(acc, index):
    rows = slice(index * 256, (index + 1) * 256)
    return behind(acc[rows, 0:128]) + acc[rows, 128:256] + ahead(acc[rows, 256:384])


class Scatter:
    def __init__(self, terms, far1, near1, mid, far2, near2, total, out, x, z, c, sems, flip):
        self.terms, self.far1, self.near1 = terms, far1, near1
        self.mid, self.far2, self.near2 = mid, far2, near2
        self.total, self.out = total, out
        self.x, self.z, self.c, self.flip = x, z, c, flip
        self.s1, self.r1, self.s2, self.r2 = sems
        self.rows = out.shape[1]

    def by_axis(self, j, act):
        if isinstance(j, int):
            return act((j + self.flip) % 2 == 0)
        x_first = lax.rem(j + self.flip, 2) == 0

        @pl.when(x_first)
        def _():
            act(True)

        @pl.when(jnp.logical_not(x_first))
        def _():
            act(False)

    def target(self, along_x, d):
        tx = lax.rem(self.x + d, 4) if along_x else self.x
        tz = self.z if along_x else lax.rem(self.z + d, 4)
        return tx * 4 + tz, self.c

    def block1(self, j, x_first, d, part=None):
        offsets = pl.ds(3 * j, 3)
        if x_first:
            lead = (offsets, lax.rem(self.x + d, 4))
            return lead if part is None else lead + (slice(2 * part, 2 * part + 2),)
        at = lax.rem(self.z + d, 4)
        return (offsets, slice(None) if part is None else slice(2 * part, 2 * part + 2), at)

    def block2(self, j, x_first, d, part=None):
        at = lax.rem((self.z if x_first else self.x) + d, 4)
        half = self.rows // 2
        lead = (j, slice(None), at)
        return lead if part is None else lead + (slice(half * part, half * (part + 1)),)

    def far(self, stage, j, x_first, way):
        src, dst = (
            (self.terms.at[self.block1(j, x_first, 2, way)], self.far1)
            if stage == 1
            else (self.mid.at[self.block2(j, x_first, 2, way)], self.far2)
        )
        s, r = (self.s1, self.r1) if stage == 1 else (self.s2, self.r2)
        to = self.target(x_first == (stage == 1), (1, 3)[way])
        return send(src, dst.at[j, way], s.at[j, way], r.at[j, way], to)

    def near(self, stage, j, x_first, way):
        step = (1, 3)[way]
        src, dst = (
            (self.terms.at[self.block1(j, x_first, step)], self.near1)
            if stage == 1
            else (self.mid.at[self.block2(j, x_first, step)], self.near2)
        )
        s, r = (self.s1, self.r1) if stage == 1 else (self.s2, self.r2)
        to = self.target(x_first == (stage == 1), step)
        return send(src, dst.at[j, way], s.at[j, 2 + way], r.at[j, 2 + way], to)

    def pass_on(self, stage, j, x_first):
        for way, step in ((0, 1), (1, 3)):
            self.far(stage, j, x_first, way).wait_recv()
            if stage == 1:
                field, got, where = self.terms, self.far1, self.block1(j, x_first, step, way)
            else:
                field, got, where = self.mid, self.far2, self.block2(j, x_first, step, way)
            field[where] = (field[where].astype(F32) + got[j, way].astype(F32)).astype(BF)
            self.near(stage, j, x_first, way).start()

    def start1(self, j):
        def act(x_first):
            self.far(1, j, x_first, 0).start()
            self.far(1, j, x_first, 1).start()

        self.by_axis(j, act)

    def relay1(self, j):
        self.by_axis(j, lambda x_first: self.pass_on(1, j, x_first))

    def start2(self, j):
        def act(x_first):
            value = self.terms[self.block1(j, x_first, 0)].astype(F32)
            for way in (0, 1):
                self.near(1, j, x_first, way).wait_recv()
                value = value + self.near1[j, way].astype(F32)
            self.total[...] = value
            self.mid[j] = value.astype(BF)
            self.far(2, j, x_first, 0).start()
            self.far(2, j, x_first, 1).start()
            self.out[pl.ds(3 * j, 3)] = self.total[:, self.z] if x_first else self.total[:, self.x]

        self.by_axis(j, act)

    def relay2(self, j):
        self.by_axis(j, lambda x_first: self.pass_on(2, j, x_first))

    def finish(self, j):
        def act(x_first):
            value = self.out[pl.ds(3 * j, 3)]
            for way in (0, 1):
                self.near(2, j, x_first, way).wait_recv()
                value = value + self.near2[j, way].astype(F32)
            self.out[pl.ds(3 * j, 3)] = value
            for stage in (1, 2):
                for way in (0, 1):
                    self.far(stage, j, x_first, way).wait_send()
                    self.near(stage, j, x_first, way).wait_send()

        self.by_axis(j, act)


def every_chunk(act, start=0, stop=9):
    def step(j, _):
        act(j)
        return 0

    lax.fori_loop(start, stop, step, 0)


def back_columns(stacked, load_w):
    total = None
    for a in range(3):
        rows = jnp.concatenate(
            [stacked[2 - a : 6 - a, 2 - b : 18 - b].reshape(1024, 384) for b in range(3)], axis=1
        )
        filters = jnp.concatenate([load_w(9 * a + k) for k in range(9)], axis=1)
        term = lax.dot_general(rows, filters, (((1,), (1,)), ((), ())), preferred_element_type=F32)
        total = term if total is None else total + term
    return total


def step_kernel(
    vol, w1, b1, w2, b2, cot,
    feat, grad_in, grad1, grad2,
    u1, u2, f1, f2, acc, slope,
    adj2, adj1, flipped2, flipped1, rim2, rim1,
    terms2, far2a, near2a, mid2, far2b, near2b, total2,
    terms1, far1a, near1a, mid1, far1b, near1b, total1,
    hid_own, hid_bf, hid_sib, hid_sum, hid_got,
    inp_own, inp_bf, inp_sib, inp_sum, inp_got,
    ag1_s, ag1_r, ag2_s, ag2_r, halo_s, halo_r, hh_s, hh_r, y_s, y_r, c_s, c_r, hy_s, hy_r, hc_s, hc_r, loc,
    g2s1, g2r1, g2s2, g2r2, g1s1, g1r1, g1s2, g1r2,
    h2s, h2r, h1s, h1r, hss, hsr, hys, hyr, iss, isr, iys, iyr,
):
    s, c, x, z, y, core = place()
    u1[0] = jnp.zeros((18, 16, 512), BF)
    u1[5] = jnp.zeros((18, 16, 512), BF)
    for row in (0, 17):
        u1[1:5, row] = jnp.zeros((4, 16, 512), BF)

    def clear(b, _):
        u2[b, 0] = jnp.zeros((18, 16, 128), BF)
        u2[b, 5] = jnp.zeros((18, 16, 128), BF)
        for row in (0, 17):
            u2[b, 1:5, row] = jnp.zeros((4, 16, 128), BF)
        return 0

    lax.fori_loop(0, 8, clear, 0)
    for field in (adj2, adj1):
        for row in (0, 17):
            field[:, row] = jnp.zeros((6, 16, 384), BF)
    for rim in (rim2, rim1):
        rim[...] = jnp.zeros_like(rim)
    rows_of = lambda cb: u1.at[:, pl.ds(1 + 2 * cb, 2)]
    locals_ = [
        pltpu.make_async_copy(vol, u1.at[1:5, pl.ds(1 + 2 * c, 2)], loc.at[0]),
        pltpu.make_async_copy(w1, f1.at[:, x, z], loc.at[1]),
        pltpu.make_async_copy(w2, f2.at[:, x, z], loc.at[2]),
    ]
    for copy in locals_:
        copy.start()
    greet(s, c, x, z)

    first = Gather(w1, f1, x, z, c, ag1_s, ag1_r, HALVES)
    second = [Gather(w2, f2, x, z, c, ag2_s.at[i], ag2_r.at[i], THIRDS[i]) for i in range(3)]
    halo = Halo(
        s, c, vol.at[0], vol.at[3],
        u1.at[0, pl.ds(1 + 2 * c, 2)], u1.at[5, pl.ds(1 + 2 * c, 2)], halo_s, halo_r,
    )
    voxels = ChanGather(rows_of, s, y, core, y_s, y_r, c_s, c_r)
    halo.start()
    first.start_own()
    locals_[0].wait()
    halo.wait_recv()
    first.near()
    voxels.start_own()
    first.relay(0)
    first.far()
    first.relay(1)
    first.relay(3)
    voxels.forward()
    first.relay(2)
    voxels.finish()
    second[0].start_own()
    second[1].start_own()
    locals_[1].wait()
    locals_[2].wait()
    acc[...] = jnp.zeros_like(acc)
    first.finish()

    hidden_halo = Halo(
        s, c, u2.at[c, 1, 1:17], u2.at[c, 4, 1:17], u2.at[c, 0, 1:17], u2.at[c, 5, 1:17], hh_s, hh_r
    )
    for a in range(3):
        convolve_part(
            lambda a, b: u1[a : a + 4, b : b + 16].reshape(1024, 512),
            lambda k: f1[k].reshape(512, 128),
            a,
            acc,
        )
        if a == 0:
            second[0].near()
    for p in (0, 3, 1, 2):
        pre = plane_of(acc, p) + b1[...]
        slope[p] = slope_of(pre)
        u2[c, p + 1, 1:17] = (pre * jax.nn.sigmoid(pre)).astype(BF).reshape(16, 16, 128)
        if p == 3:
            hidden_halo.start()
            second[2].start_own()
    channels, low_rim, high_rim = [
        ChanGather(
            lambda cb, planes=planes: u2.at[cb, planes, 1:17],
            s, y, core, hy_s.at[i], hy_r.at[i], hc_s.at[i], hc_r.at[i],
        )
        for i, planes in enumerate((slice(1, 5), 0, 5))
    ]
    channels.start_own()
    second[0].relay(3)
    second[1].near()
    acc[...] = jnp.zeros_like(acc)
    second[2].near()
    hidden_halo.wait_recv()
    low_rim.start_own()
    high_rim.start_own()
    second[0].far()
    second[0].relay(0)
    second[1].far()
    channels.forward()
    second[0].relay(1)
    second[1].relay(0)
    second[0].relay(2)
    second[1].relay(3)
    low_rim.forward()
    high_rim.forward()
    second[1].relay(1)
    second[2].far()
    channels.finish()
    low_rim.finish()
    high_rim.finish()
    second[1].relay(2)
    second[2].relay(3)
    second[2].relay(1)
    second[0].finish()
    second[2].relay(0)
    for a in range(3):
        convolve_part(
            lambda a, b: jnp.concatenate(
                [u2[q, a : a + 4, b : b + 16].reshape(1024, 128) for q in range(8)], axis=1
            ),
            lambda k: f2[k].reshape(1024, 128),
            a,
            acc,
        )
        if a < 2:
            second[a + 1].finish()
        if a == 0:
            second[2].relay(2)
    middle = slice(128, 256)
    halo2 = Halo(
        s, c, adj2.at[1, 1:17, :, middle], adj2.at[4, 1:17, :, middle], rim2.at[0], rim2.at[1], h2s, h2r
    )
    for p in (0, 3, 1, 2):
        pre = plane_of(acc, p) + b2[...]
        feat[p] = (pre * jax.nn.sigmoid(pre)).astype(BF).reshape(16, 16, 128)
        adjoint = cot[p].reshape(256, 128).astype(F32) * slope_of(pre)
        stack_shifts(adjoint, p, adj2, 1, 1, flipped2)
        if p == 3:
            halo2.start()
    sibling = (s, y * 2 + 1 - core)

    def take_rims(halo, rim, field):
        halo.wait_recv()
        for side, plane in ((0, 0), (1, 5)):
            stack_shifts(rim[side].reshape(256, 128).astype(F32), plane, field, 0, 1)

    scatter2 = Scatter(
        terms2, far2a, near2a, mid2, far2b, near2b, total2, grad2, x, z, c, (g2s1, g2r1, g2s2, g2r2), 0
    )
    scatter1 = Scatter(
        terms1, far1a, near1a, mid1, far1b, near1b, total1, grad1, x, z, c, (g1s1, g1r1, g1s2, g1r2), 1
    )

    def second_chunk(j):
        a, b = lax.div(j, 3), lax.rem(j, 3)

        fields = [u2[q, pl.ds(a, 4), pl.ds(b, 16)].reshape(1024, 128) for q in range(8)]
        turned = dot(flipped2[...], jnp.concatenate(fields, axis=1)).T.astype(BF)
        for k in range(3):
            terms2[3 * j + k] = turned[:, k * 128 : (k + 1) * 128].reshape(4, 4, 64, 128)
        scatter2.start1(j)

    every_chunk(second_chunk, 0, 6)
    scatter2.relay1(0)
    scatter2.relay1(1)
    take_rims(halo2, rim2, adj2)

    def hidden_to_sibling(n):
        return send(hid_bf.at[n, 1 - core], hid_sib.at[n], hss.at[n], hsr.at[n], sibling)

    def hidden_to_y(d):
        n = lax.rem(y + d, 4)
        return send(hid_sum.at[n], hid_got.at[d - 1], hys.at[d - 1], hyr.at[d - 1], (s, n * 2 + core))

    def hidden_pair(n):
        hidden_to_sibling(n).wait_recv()
        return hid_own[n] + hid_sib[n].astype(F32)

    def hidden_columns(i, _):
        n = lax.rem(y + 1 + i, 4)
        pl.when(i < 3)(lambda: second_chunk(jnp.minimum(6 + i, 8)))

        @pl.when(i == 1)
        def _():
            scatter2.relay1(3)

        value = back_columns(adj2, lambda k: f2[k, n].reshape(256, 128))
        low, high = value[:, :128], value[:, 128:]
        hid_bf[n, 0] = low.astype(BF)
        hid_bf[n, 1] = high.astype(BF)
        hid_own[n] = jnp.where(core == 0, low, high)
        hidden_to_sibling(n).start()

        @pl.when(i > 0)
        def _():
            d = jnp.maximum(i, 1)
            before = lax.rem(y + d, 4)
            hid_sum[before] = hidden_pair(before).astype(BF)
            hidden_to_y(d).start()

        @pl.when(i == 0)
        def _():
            scatter2.relay1(2)

        @pl.when(i == 2)
        def _():
            scatter2.start2(0)
            scatter2.relay1(4)
            scatter2.relay1(5)
            scatter2.relay1(6)
            scatter2.relay1(7)

        return 0

    lax.fori_loop(0, 4, hidden_columns, 0)
    hid_own[y] = hidden_pair(y)

    scatter2.start2(1)
    scatter2.start2(2)
    scatter2.start2(3)
    scatter2.start2(4)
    scatter2.relay1(8)
    scatter2.relay2(0)
    for d in RING:
        hidden_to_y(d).wait_recv()
    for p in range(4):
        rows = slice(p * 256, (p + 1) * 256)
        value = hid_own[y, rows]
        for d in range(3):
            value = value + hid_got[d, rows].astype(F32)
        stack_shifts(value * slope[p], p, adj1, 1, 1, flipped1)
    halo1 = Halo(
        s, c, adj1.at[1, 1:17, :, middle], adj1.at[4, 1:17, :, middle], rim1.at[0], rim1.at[1], h1s, h1r
    )
    halo1.start()

    def first_chunk(j):
        a, b = lax.div(j, 3), lax.rem(j, 3)
        field = u1[pl.ds(a, 4), pl.ds(b, 16)].reshape(1024, 512)
        turned = dot(flipped1[...], field).T.astype(BF)
        for k in range(3):
            terms1[3 * j + k] = turned[:, k * 128 : (k + 1) * 128].reshape(4, 4, 32, 128)
        scatter1.start1(j)

    def first_step(j):
        first_chunk(j)

        @pl.when(j == 0)
        def _():
            scatter2.relay2(1)

        @pl.when(j == 1)
        def _():
            scatter2.relay2(2)

        @pl.when(j == 5)
        def _():
            scatter1.relay1(0)

        @pl.when(j == 7)
        def _():
            scatter2.start2(5)
            scatter1.relay1(1)
            scatter1.relay1(2)

    every_chunk(first_step)
    scatter1.relay1(3)
    scatter1.relay1(4)
    take_rims(halo1, rim1, adj1)
    for n in range(2):
        value = back_columns(adj1, lambda k: f1[k, 2 * n : 2 * n + 2].reshape(256, 128))
        value = value.reshape(4, 4, 2, 2, 16, 256)
        columns = slice(n * 256, (n + 1) * 256)
        inp_own[:, :, :, :, :, columns] = value
        inp_bf[:, :, :, :, :, columns] = value.astype(BF)
        if n == 0:
            scatter1.relay1(5)
            scatter1.start2(0)
            scatter1.relay1(6)
    to_sibling = send(inp_bf.at[:, :, 1 - core], inp_sib, iss.at[0], isr.at[0], sibling)
    to_sibling.start()

    def input_to_y(d):
        n = lax.rem(y + d, 4)
        return send(inp_sum.at[n], inp_got.at[d - 1], iys.at[d - 1], iyr.at[d - 1], (s, n * 2 + core))

    scatter1.relay1(7)
    scatter2.relay2(3)
    scatter2.start2(6)
    scatter1.relay1(8)
    scatter1.start2(1)
    scatter1.start2(2)
    scatter1.start2(3)
    scatter2.start2(7)
    scatter2.relay2(4)
    scatter2.finish(0)
    scatter1.start2(4)
    to_sibling.wait_recv()
    for d in (1, 3, 2, 0):
        n = lax.rem(y + d, 4)
        pair = inp_own[:, n, core] + inp_sib[:, n].astype(F32)
        if d:
            inp_sum[n] = pair.astype(BF)
            input_to_y(d).start()
        else:
            grad_in[...] = pair
    scatter1.start2(5)
    scatter1.start2(6)
    scatter2.relay2(5)
    scatter1.start2(7)
    scatter2.start2(8)
    scatter2.relay2(6)
    scatter2.finish(1)
    scatter2.finish(2)
    scatter1.relay2(0)
    scatter1.start2(8)
    scatter1.relay2(1)
    scatter1.relay2(2)
    scatter1.relay2(3)
    scatter1.relay2(4)
    scatter2.relay2(7)
    scatter2.finish(3)
    scatter1.relay2(5)
    scatter1.relay2(6)
    scatter1.relay2(7)
    scatter2.relay2(8)
    scatter1.finish(0)
    scatter1.relay2(8)
    scatter2.finish(4)
    scatter1.finish(1)
    scatter1.finish(2)
    scatter1.finish(3)
    scatter2.finish(5)
    scatter2.finish(6)
    scatter1.finish(4)
    scatter1.finish(5)
    for d in RING:
        input_to_y(d).wait_recv()
    value = grad_in[...]
    for d in range(3):
        value = value + inp_got[d].astype(F32)
    grad_in[...] = value
    scatter1.finish(6)
    scatter1.finish(7)
    scatter2.finish(7)
    scatter1.finish(8)
    scatter2.finish(8)

    halo2.wait_send()
    halo1.wait_send()
    to_sibling.wait_send()
    for n in range(4):
        hidden_to_sibling(n).wait_send()
    for d in RING:
        hidden_to_y(d).wait_send()
        input_to_y(d).wait_send()
    halo.wait_send()
    hidden_halo.wait_send()
    voxels.wait_send()
    for part in (channels, low_rim, high_rim):
        part.wait_send()
    first.wait_send()
    for part in second:
        part.wait_send()


def hand_over(*refs):
    for i in range(4):
        refs[4 + i][...] = refs[i][...]


def vmem(count):
    return [pl.BlockSpec(memory_space=pltpu.VMEM)] * count


def anywhere(count):
    return [pl.BlockSpec(memory_space=pl.ANY)] * count


def dma(*shape):
    return pltpu.SemaphoreType.DMA(shape)


def local(volume, w_first, b_first, w_second, b_second, cotangent):
    shape = jax.ShapeDtypeStruct
    flops = 2 * 1024 * 27 * 128 * 1536
    half_banks = lambda rows: [
        pltpu.VMEM((27, 4, 4, rows, 128), BF),
        pltpu.VMEM((9, 2, 3, 2, rows, 128), BF),
        pltpu.VMEM((9, 2, 3, 4, rows, 128), BF),
        pltpu.VMEM((9, 3, 4, rows, 128), BF),
        pltpu.VMEM((9, 2, 3, rows // 2, 128), BF),
        pltpu.VMEM((9, 2, 3, rows, 128), BF),
        pltpu.VMEM((3, 4, rows, 128), F32),
    ]
    features, grad_input, grad_first, grad_second = pl.pallas_call(
        step_kernel,
        name="forward_backward",
        out_shape=(
            shape((4, 16, 16, 128), BF),
            shape((4, 2, 16, 512), F32),
            shape((27, 32, 128), F32),
            shape((27, 64, 128), F32),
        ),
        in_specs=vmem(1) + anywhere(1) + vmem(1) + anywhere(1) + vmem(2),
        out_specs=tuple(vmem(4)),
        scratch_shapes=[
            pltpu.VMEM((6, 18, 16, 512), BF),
            pltpu.VMEM((8, 6, 18, 16, 128), BF),
            pltpu.VMEM((27, 4, 4, 32, 128), BF),
            pltpu.VMEM((27, 4, 4, 64, 128), BF),
            pltpu.VMEM((1024, 384), F32),
            pltpu.VMEM((4, 256, 128), F32),
            pltpu.VMEM((6, 18, 16, 384), BF),
            pltpu.VMEM((6, 18, 16, 384), BF),
            pltpu.VMEM((384, 1024), BF),
            pltpu.VMEM((384, 1024), BF),
            pltpu.VMEM((2, 16, 16, 128), BF),
            pltpu.VMEM((2, 16, 16, 128), BF),
            *half_banks(64),
            *half_banks(32),
            pltpu.VMEM((4, 1024, 128), F32),
            pltpu.VMEM((4, 2, 1024, 128), BF),
            pltpu.VMEM((4, 1024, 128), BF),
            pltpu.VMEM((4, 1024, 128), BF),
            pltpu.VMEM((3, 1024, 128), BF),
            pltpu.VMEM((4, 4, 2, 2, 16, 512), F32),
            pltpu.VMEM((4, 4, 2, 2, 16, 512), BF),
            pltpu.VMEM((4, 4, 2, 16, 512), BF),
            pltpu.VMEM((4, 4, 2, 16, 512), BF),
            pltpu.VMEM((3, 4, 2, 16, 512), BF),
            dma(2, 5, 4), dma(2, 5, 4), dma(3, 2, 5, 4), dma(3, 2, 5, 4),
            dma(2), dma(2), dma(2), dma(2),
            dma(4), dma(4), dma(4), dma(4), dma(3, 4), dma(3, 4), dma(3, 4), dma(3, 4),
            dma(3),
            dma(9, 4), dma(9, 4), dma(9, 4), dma(9, 4),
            dma(9, 4), dma(9, 4), dma(9, 4), dma(9, 4),
            dma(2), dma(2), dma(2), dma(2),
            dma(4), dma(4), dma(3), dma(3),
            dma(1), dma(1), dma(3), dma(3),
        ],
        compiler_params=pltpu.CompilerParams(
            collective_id=0, has_side_effects=True, vmem_limit_bytes=VMEM_BYTES
        ),
        cost_estimate=pl.CostEstimate(flops=3 * flops, bytes_accessed=8_000_000, transcendentals=600_000),
    )(volume, w_first, b_first.reshape(1, 128), w_second, b_second.reshape(1, 128), cotangent)
    results = (features, grad_input, grad_first, grad_second)
    return pl.pallas_call(
        hand_over,
        name="hand_over",
        out_shape=tuple(shape(r.shape, r.dtype) for r in results),
        in_specs=vmem(4),
        out_specs=tuple(vmem(4)),
        compiler_params=pltpu.CompilerParams(vmem_limit_bytes=VMEM_BYTES),
    )(*results)


def solution(mesh):
    return jax.shard_map(
        local,
        mesh=mesh,
        in_specs=(
            P("space", "chan", None, None),
            P(None, "space", "chan"),
            P("chan"),
            P(None, "space", "chan"),
            P("chan"),
            P("space", None, None, "chan"),
        ),
        out_specs=(
            P("space", None, None, "chan"),
            P("space", "chan", None, None),
            P(None, "space", "chan"),
            P(None, "space", "chan"),
        ),
        check_vma=False,
    )
```
